512 devices in a mesh: bx: 16 (over z_hi, y), by: 32 (over z_lo, x, core).
Axes of the slice: x: 4, y: 4, z: 16 (z_hi: 4, z_lo: 4; z = z_hi * 4 + z_lo), core: 2. Of those that a mesh axis runs over, the one named last changes fastest.
Arguments:
- density: float32 [512, 1024, 128], P('bx', 'by'), may hold values from 0 to 6
- band_feat: bfloat16 [16, 32, 4, 2048, 64], P('bx', 'by'), may hold values from -6 to 6
- band_cell: int32 [16, 32, 4, 2048], P('bx', 'by'), may hold values from 0 to 131071, as said below
- band_count: int32 [16, 32, 4], P('bx', 'by'), may hold values from 1024 to 2048, as said below
- w_in: bfloat16 [16, 32, 64, 256], P('bx', 'by'), may hold values from -0.75 to 0.75
- w_hid: bfloat16 [16, 32, 4, 256, 256], P('bx', 'by'), may hold values from -0.5 to 0.5
- w_out: bfloat16 [16, 32, 256], P('bx', 'by'), may hold values from -0.5 to 0.5
- biases: float32 [16, 32, 5, 256], P('bx', 'by'), may hold values from -2 to 2
Outputs:
- smoothed: float32 [512, 1024, 128], P('bx', 'by')
- normals: float32 [3, 512, 1024, 128], P(None, 'bx', 'by')
The draws below stay inside these ranges and needn't reach their ends.
Inputs may be any that keep to these rules, and one draw needn't show every extreme that they name: `band_count`: every count is 1024 or more, and some side of some block reaches 2048. `band_cell`: the entries of one side of one block are voxels of that side's band, the 16 voxels next to the block's face: side 0 at the low end of the first dimension, 1 at its high end, 2 and 3 likewise along the second. Taking the band's voxels in row-major order of the band itself (first dimension, second, height) and cutting that order into 2048 equal consecutive runs, entry r lies in run r.
All inputs are finite; a program needn't handle non-finite values.
Results may differ from the reference program's by a relative error of at most 0.0008.
Values may be sent and summed in bfloat16 or wider, within the bound.
A program may use at most 64 MiB of HBM per device.

```python
import jax
import jax.numpy as jnp
from jax import lax

CX = 32
CY = 32
CZ = 128
W = 16
CAP = 2048
F = 64
H = 256
LH = 4
NX = 512
NY = 1024
N_BX = 16
N_BY = 32


def draw_band_count(key, part):
    key = jax.random.fold_in(key, 11)
    key_one, key_two = jax.random.split(key, 2)
    counts = CAP // 2 + jax.random.randint(key_one, (N_BX, N_BY, 4), 0, CAP - CAP // 2 + 1)
    chosen = jax.random.randint(key_two, (), 0, N_BX * N_BY * 4)
    return counts.reshape(-1).at[chosen].set(CAP).reshape(N_BX, N_BY, 4).astype(jnp.int32)


def draw_band_cell(key, part):
    key = jax.random.fold_in(key, 23)
    key_one, key_two = jax.random.split(key, 2)
    slot_x = W * CY * CZ // CAP
    slot_y = CX * W * CZ // CAP
    ranks = jnp.arange(CAP, dtype=jnp.int32)
    pos_one = ranks * slot_x + jax.random.randint(key_one, (N_BX, N_BY, 2, CAP), 0, slot_x)
    lift_x = jnp.array([0, CX - W], dtype=jnp.int32)[None, None, :, None]
    cell_one = (pos_one // (CY * CZ) + lift_x) * (CY * CZ) + pos_one % (CY * CZ)
    pos_two = ranks * slot_y + jax.random.randint(key_two, (N_BX, N_BY, 2, CAP), 0, slot_y)
    lift_y = jnp.array([0, CY - W], dtype=jnp.int32)[None, None, :, None]
    across = pos_two // (W * CZ)
    along = pos_two // CZ % W + lift_y
    cell_two = (across * CY + along) * CZ + pos_two % CZ
    return jnp.concatenate([cell_one, cell_two], axis=2).astype(jnp.int32)


def shard_levels(stream_key, extent, pieces, smallest, top_value):
    def one(dim, parts):
        steps = jax.random.uniform(jax.random.fold_in(jax.random.fold_in(stream_key, 6), dim), (parts,), jnp.float32, smallest / len(pieces), top_value / len(pieces))
        return jnp.repeat(jnp.exp(steps), extent[dim] // parts).reshape((-1,) + (1,) * (len(extent) - dim - 1))

    gain = one(*pieces[0])
    for cut in pieces[1:]:
        gain = gain * one(*cut)
    return gain


def scatter_about(rng, dims, width, limit, shards=(), held_as=jnp.bfloat16):
    values = jax.random.normal(rng, dims, jnp.float32) * width
    if len(shards) > 0:
        values = shard_levels(rng, dims, shards, -0.22, 0.18) * values
    return jnp.clip(values, min=-limit, max=limit).astype(held_as)


def setup_inputs(seed: int = 0) -> dict:
    splits = jax.random.split(jax.random.key(seed), 9)
    density = jnp.clip(6.0 * jax.random.uniform(splits[0], (NX, NY, CZ), jnp.float32) ** shard_levels(splits[0], (NX, NY, CZ), ((0, 16), (1, 32)), -0.2, 0.2), 0.0, 6.0)
    band_feat = scatter_about(splits[1], (N_BX, N_BY, 4, CAP, F), 1.0, 6.0, ((0, 16), (1, 32)))
    band_cell = draw_band_cell(jax.random.fold_in(splits[8], 71), 0)
    band_count = draw_band_count(jax.random.fold_in(splits[8], 71), 0)
    w_in = scatter_about(splits[4], (N_BX, N_BY, F, H), F ** -0.5, 0.75, ((0, 16), (1, 32)))
    w_hid = scatter_about(splits[5], (N_BX, N_BY, LH, H, H), (H // 2) ** -0.5, 0.5, ((0, 16), (1, 32)))
    w_out = scatter_about(splits[6], (N_BX, N_BY, H), (H // 2) ** -0.5, 0.5, ((0, 16), (1, 32)))
    biases = scatter_about(splits[7], (N_BX, N_BY, LH + 1, H), 0.3, 2.0, ((0, 16), (1, 32)), jnp.float32)
    return dict(density=density, band_feat=band_feat, band_cell=band_cell, band_count=band_count, w_in=w_in, w_hid=w_hid, w_out=w_out, biases=biases)


OFFSETS = ((-1, 0), (1, 0), (0, -1), (0, 1))

def network(features, w_in, w_hid, w_out, biases):
    hidden = jnp.maximum(jnp.dot(features, w_in, preferred_element_type=jnp.float32) + biases[0], 0.0).astype(jnp.bfloat16)
    for levels in range(w_hid.shape[0]):
        hidden = jnp.maximum(jnp.dot(hidden, w_hid[levels], preferred_element_type=jnp.float32) + biases[levels + 1], 0.0).astype(jnp.bfloat16)
    return jax.nn.softplus(jnp.dot(hidden, w_out, preferred_element_type=jnp.float32))

def weight_at(cell_index, tile_x, tile_y, tile_z, off_x, off_y):
    pos_x = (cell_index // (tile_y * tile_z)).astype(jnp.float32)
    pos_y = (cell_index // tile_z % tile_y).astype(jnp.float32)
    delta_x = (pos_x + 0.5) / tile_x - 0.5 - off_x
    delta_y = (pos_y + 0.5) / tile_y - 0.5 - off_y
    return 1.0 / (delta_x * delta_x + delta_y * delta_y + 0.25)

def smooth_once(padded):
    return (padded[1:-1, 1:-1] + padded[2:, 1:-1] + padded[:-2, 1:-1] + padded[1:-1, 2:] + padded[1:-1, :-2]) / 5.0

def reference(density, band_feat, band_cell, band_count, w_in, w_hid, w_out, biases):
    grid_x = N_BX
    grid_y = N_BY
    cells = CX * CY * CZ
    tile_rows = density.reshape(grid_x, CX, grid_y, CY, CZ).transpose(0, 2, 1, 3, 4).reshape(grid_x * grid_y, cells)
    every_cell = jnp.arange(cells, dtype=jnp.int32)
    own_weight = weight_at(every_cell, CX, CY, CZ, 0.0, 0.0)

    def one_block(block):
        row_block = block // grid_y
        col_block = block % grid_y
        numerator = jnp.zeros((cells,), jnp.float32)
        denominator = jnp.zeros((cells,), jnp.float32)
        for facing in range(4):
            off_x, off_y = OFFSETS[facing]
            near_x = row_block + off_x
            near_y = col_block + off_y
            exists = (near_x >= 0) & (near_x < grid_x) & (near_y >= 0) & (near_y < grid_y)
            near_x = jnp.clip(near_x, 0, grid_x - 1)
            near_y = jnp.clip(near_y, 0, grid_y - 1)
            remote = network(band_feat[row_block, col_block, facing], w_in[near_x, near_y], w_hid[near_x, near_y], w_out[near_x, near_y], biases[near_x, near_y])
            cell_index = band_cell[row_block, col_block, facing]
            usable = (jnp.arange(CAP, dtype=jnp.int32) < band_count[row_block, col_block, facing]) & exists
            weight = jnp.where(usable, weight_at(cell_index, CX, CY, CZ, float(off_x), float(off_y)), 0.0)
            numerator = numerator.at[cell_index].add(weight * remote)
            denominator = denominator.at[cell_index].add(weight)
        return (own_weight * tile_rows[block] + numerator) / (own_weight + denominator)
    blended = lax.map(one_block, jnp.arange(grid_x * grid_y, dtype=jnp.int32))
    smoothed = blended.reshape(grid_x, grid_y, CX, CY, CZ).transpose(0, 2, 1, 3, 4).reshape(grid_x * CX, grid_y * CY, CZ)
    for passes in range(3):
        smoothed = smooth_once(jnp.pad(smoothed, ((1, 1), (1, 1), (0, 0))))
    padded = jnp.pad(smoothed, ((1, 1), (1, 1), (0, 0)))
    grad_x = padded[2:, 1:-1] - padded[:-2, 1:-1]
    grad_y = padded[1:-1, 2:] - padded[1:-1, :-2]
    padded_z = jnp.pad(smoothed, ((0, 0), (0, 0), (1, 1)))
    grad_z = padded_z[:, :, 2:] - padded_z[:, :, :-2]
    factor = 1.0 / jnp.sqrt(1.0 + grad_x * grad_x + grad_y * grad_y + grad_z * grad_z)
    normals = jnp.stack([grad_x * factor, grad_y * factor, grad_z * factor])
    return (smoothed, normals)
```

```python
import functools

import jax
import jax.numpy as jnp
from jax import lax
from jax.experimental import pallas as pl
from jax.experimental.pallas import tpu as pltpu
from jax.sharding import PartitionSpec as P

MESH = pl.DeviceIdType.MESH
F32, BF16, I32 = jnp.float32, jnp.bfloat16, jnp.int32
HX, HY = 4, 8
AROUND = ((-1, 0), (1, 0), (0, -1), (0, 1), (-1, -1), (-1, 1), (1, -1), (1, 1))


def spread(row, index):
    wide = jnp.broadcast_to(row, index.shape)
    return jnp.take_along_axis(wide, index, axis=1, mode="promise_in_bounds")


def blend_kernel(
    dens, feat, cell, count, w_in, w_hid, w_out, bias, out,
    ext, recv, values, back, cells, coef_x, coef_y, win_t, whid_t, bias_w,
    feat_send, feat_recv, back_send, back_recv, halo_send, halo_recv, out_sem,
):
    ix, iy = lax.axis_index("bx"), lax.axis_index("by")
    nx, ny = lax.axis_size("bx"), lax.axis_size("by")
    size_x, size_y, size_z = dens.shape
    listed = cell.shape[1]
    rows = listed // 128

    def there(dx, dy):
        ok_x = jnp.bool_(True) if dx == 0 else (ix + dx >= 0 if dx < 0 else ix + dx < nx)
        ok_y = jnp.bool_(True) if dy == 0 else (iy + dy >= 0 if dy < 0 else iy + dy < ny)
        return ok_x & ok_y

    def at(dx, dy):
        return {"bx": ix + dx, "by": iy + dy}

    ext[...] = jnp.zeros_like(ext)
    back[...] = jnp.zeros_like(back)
    barrier = pltpu.get_barrier_semaphore()
    for dx, dy in AROUND:
        @pl.when(there(dx, dy))
        def _(dx=dx, dy=dy):
            pl.semaphore_signal(barrier, inc=1, device_id=at(dx, dy), device_id_type=MESH)

    for layer in range(w_hid.shape[0]):
        whid_t[layer] = w_hid[layer].T
    win_t[...] = w_in[...].T
    for layer in range(bias.shape[0]):
        column = jnp.broadcast_to(bias[layer : layer + 1, :], (128, bias.shape[1])).T
        bias_w[layer] = column
    ranks = lax.broadcasted_iota(I32, (1, listed), 1)
    for s in range(4):
        usable = (ranks < count[s]) & there(*AROUND[s])
        height = jnp.where(usable, cell[s : s + 1, :] & (size_z - 1), -1)
        for r in range(rows):
            cells[s * rows + r : s * rows + r + 1, :] = height[:, r * 128 : (r + 1) * 128]

    lane = lax.broadcasted_iota(I32, (8, 128), 1)
    sub = lax.broadcasted_iota(I32, (8, 128), 0)
    groups = size_y // 8
    index = [4 * (8 * g + sub) + lane // 32 for g in range(groups)]
    dist_y = [((8 * g + sub).astype(F32) + 0.5) / size_y - 0.5 for g in range(groups)]

    def list_rows(table, x, pair, parity):
        row_x = table[pl.ds(x, 1), :]
        row_2 = table[pl.ds(2 * rows + pair, 1), :]
        row_3 = table[pl.ds(3 * rows + pair, 1), :]
        along_x = [spread(row_x, index[g]) for g in range(groups)]
        half = groups // 2
        along_y = [spread(row_2 if g < half else row_3, index[g % half + half * parity]) for g in range(groups)]
        return along_x, along_y

    def prepare(pair, _):
        for parity in range(2):
            x = 2 * pair + parity
            dist_x = (x.astype(F32) + 0.5) / size_x - 0.5
            off_x = jnp.where(x < size_x // 2, -1.0, 1.0)
            along_x, along_y = list_rows(cells, x, pair, parity)
            for g in range(groups):
                off_y = -1.0 if g < groups // 2 else 1.0
                sq_x, sq_y = dist_x * dist_x, dist_y[g] * dist_y[g]
                far_x, far_y = dist_x - off_x, dist_y[g] - off_y
                own = 1.0 / (sq_x + sq_y + 0.25)
                w_x = jnp.where(along_x[g] == lane, 1.0 / (far_x * far_x + sq_y + 0.25), 0.0)
                w_y = jnp.where(along_y[g] == lane, 1.0 / (sq_x + far_y * far_y + 0.25), 0.0)
                share = 1.0 / (own + w_x + w_y)
                voxels = pl.ds(8 * g, 8)
                ext[HX + x, pl.ds(HY + 8 * g, 8), :] = own * dens[x, voxels, :] * share
                coef_x[x, voxels, :] = w_x * share
                coef_y[x, voxels, :] = w_y * share
        return 0

    lax.fori_loop(0, size_x // 2, prepare, 0)

    pl.semaphore_wait(barrier, sum(there(dx, dy).astype(I32) for dx, dy in AROUND))

    def opposite(s):
        dx = jnp.where(s == 0, 1, jnp.where(s == 1, -1, 0))
        dy = jnp.where(s == 2, 1, jnp.where(s == 3, -1, 0))
        ok = (ix + dx >= 0) & (ix + dx < nx) & (iy + dy >= 0) & (iy + dy < ny)
        return ok, dx, dy

    def feature_copy(s, dx, dy):
        return pltpu.make_async_remote_copy(
            src_ref=feat.at[s], dst_ref=recv.at[s], send_sem=feat_send.at[s], recv_sem=feat_recv.at[s],
            device_id=at(dx, dy), device_id_type=MESH)

    for s in range(4):
        @pl.when(there(*AROUND[s]))
        def _(s=s):
            feature_copy(s, *AROUND[s]).start()

    def value_copy(s, dx, dy):
        return pltpu.make_async_remote_copy(
            src_ref=values.at[s], dst_ref=back.at[s], send_sem=back_send.at[s], recv_sem=back_recv.at[s],
            device_id=at(dx, dy), device_id_type=MESH)

    head = jnp.broadcast_to(w_out[...].astype(F32), (16, w_out.shape[1])).astype(BF16)
    last = ix % 4 == 3

    def evaluate(step, _):
        s = jnp.where(step < 2, step + 2, jnp.where(last, 3 - step, step - 2))
        ok, dx, dy = opposite(s)

        @pl.when(ok)
        def _():
            feature_copy(s, dx, dy).wait_recv()

            def layer(weights, hidden, level):
                wide = jnp.concatenate([bias_w[level]] * (listed // 128), axis=1)
                total = jnp.dot(weights, hidden, preferred_element_type=F32) + wide
                return jnp.maximum(total.astype(BF16), 0)

            hidden = layer(win_t[...], recv[s], 0)
            for level in range(whid_t.shape[0]):
                hidden = layer(whid_t[level], hidden, level + 1)
            raw = jnp.dot(head, hidden, preferred_element_type=F32)[0:1, :]
            result = jnp.maximum(raw, 0.0) + jnp.log1p(jnp.exp(-jnp.abs(raw)))
            for r in range(rows):
                values[s, r : r + 1, :] = result[:, r * 128 : (r + 1) * 128]
            value_copy(s, dx, dy).start()

        return 0

    lax.fori_loop(0, 4, evaluate, 0)

    for s in range(4):
        @pl.when(there(*AROUND[s]))
        def _(s=s):
            value_copy(s, *AROUND[s]).wait_recv()

    def blend(pair, _):
        for parity in range(2):
            x = 2 * pair + parity
            side_x = pair // (rows // 2)
            row_x = back[side_x, pl.ds(x - side_x * rows, 1), :]
            row_2 = back[2, pl.ds(pair, 1), :]
            row_3 = back[3, pl.ds(pair, 1), :]
            half = groups // 2
            for g in range(groups):
                voxels = pl.ds(8 * g, 8)
                at_x = spread(row_x, index[g])
                at_y = spread(row_2 if g < half else row_3, index[g % half + half * parity])
                place = pl.ds(HY + 8 * g, 8)
                ext[HX + x, place, :] = (
                    ext[HX + x, place, :] + coef_x[x, voxels, :] * at_x + coef_y[x, voxels, :] * at_y
                )
        return 0

    lax.fori_loop(0, size_x // 2, blend, 0)

    def halo_copy(n, dx, dy):
        def cut(d, own, width, inner):
            if d == 0:
                return pl.ds(own, inner), pl.ds(own, inner)
            if d > 0:
                return pl.ds(own + inner - width, width), pl.ds(own - width, width)
            return pl.ds(own, width), pl.ds(own + inner, width)

        src_x, dst_x = cut(dx, HX, HX, size_x)
        src_y, dst_y = cut(dy, HY, HY, size_y)
        return pltpu.make_async_remote_copy(
            src_ref=ext.at[src_x, src_y, :], dst_ref=ext.at[dst_x, dst_y, :],
            send_sem=halo_send.at[n], recv_sem=halo_recv.at[n],
            device_id=at(dx, dy), device_id_type=MESH)

    for n, (dx, dy) in enumerate(AROUND):
        @pl.when(there(dx, dy))
        def _(n=n, dx=dx, dy=dy):
            halo_copy(n, dx, dy).start()

    for s in range(4):
        @pl.when(there(*AROUND[s]))
        def _(s=s):
            feature_copy(s, *AROUND[s]).wait_send()

        @pl.when(there(-AROUND[s][0], -AROUND[s][1]))
        def _(s=s):
            value_copy(s, -AROUND[s][0], -AROUND[s][1]).wait_send()

    for n, (dx, dy) in enumerate(AROUND):
        @pl.when(there(-dx, -dy))
        def _(n=n, dx=dx, dy=dy):
            halo_copy(n, -dx, -dy).wait_recv()

        @pl.when(there(dx, dy))
        def _(n=n, dx=dx, dy=dy):
            halo_copy(n, dx, dy).wait_send()

    copy = pltpu.make_async_copy(ext, out, out_sem)
    copy.start()
    copy.wait()


def finish_kernel(ext, smoothed, normals, one, two):
    ix, iy = lax.axis_index("bx"), lax.axis_index("by")
    nx, ny = lax.axis_size("bx"), lax.axis_size("by")
    size_x, size_y, size_z = smoothed.shape
    full_x, full_y = size_x + 2 * HX, size_y + 2 * HY
    sub = lax.broadcasted_iota(I32, (full_y, size_z), 0)
    inside_y = ((sub >= HY) | (iy > 0)) & ((sub < HY + size_y) | (iy < ny - 1))
    keep_y = jnp.where(inside_y, 0.2, 0.0)

    def one_pass(src, dst, margin):
        def step(x, _):
            centre = src[x]
            total = (
                centre + src[x + 1] + src[x - 1]
                + pltpu.roll(centre, 1, 0) + pltpu.roll(centre, full_y - 1, 0)
            )
            inside = ((x >= HX) | (ix > 0)) & ((x < HX + size_x) | (ix < nx - 1))
            dst[x] = total * jnp.where(inside, keep_y, 0.0)
            return 0

        lax.fori_loop(margin, full_x - margin, step, 0, unroll=2)

    one_pass(ext, one, 1)
    one_pass(one, two, 2)
    one_pass(two, one, 3)
    last_z = lax.broadcasted_iota(I32, (size_y, size_z), 1)

    def gradient(x, _):
        row = HX + x
        centre = one[row]
        own = centre[HY : HY + size_y]
        grad_x = one[row + 1, HY : HY + size_y, :] - one[row - 1, HY : HY + size_y, :]
        grad_y = (pltpu.roll(centre, full_y - 1, 0) - pltpu.roll(centre, 1, 0))[HY : HY + size_y]
        after = jnp.where(last_z == size_z - 1, 0.0, pltpu.roll(own, size_z - 1, 1))
        before = jnp.where(last_z == 0, 0.0, pltpu.roll(own, 1, 1))
        grad_z = after - before
        factor = lax.rsqrt(1.0 + grad_x * grad_x + grad_y * grad_y + grad_z * grad_z)
        smoothed[x] = own
        normals[0, x] = grad_x * factor
        normals[1, x] = grad_y * factor
        normals[2, x] = grad_z * factor
        return 0

    lax.fori_loop(0, size_x, gradient, 0, unroll=2)


def shards(density, band_feat, band_cell, band_count, w_in, w_hid, w_out, biases):
    size_x, size_y, size_z = density.shape
    feat = jnp.swapaxes(band_feat[0, 0], 1, 2)
    sides, width, listed = feat.shape
    levels, hidden = w_hid.shape[2], w_hid.shape[3]
    rows = listed // 128
    full = (size_x + 2 * HX, size_y + 2 * HY, size_z)
    vmem = pl.BlockSpec(memory_space=pltpu.VMEM)
    dma = pltpu.SemaphoreType.DMA
    ext = pl.pallas_call(
        blend_kernel,
        out_shape=jax.ShapeDtypeStruct(full, F32),
        in_specs=[vmem, pl.BlockSpec(memory_space=pl.ANY), vmem, pl.BlockSpec(memory_space=pltpu.SMEM)] + [vmem] * 4,
        out_specs=pl.BlockSpec(memory_space=pl.ANY),
        scratch_shapes=[
            pltpu.VMEM(full, F32),
            pltpu.VMEM((sides, width, listed), BF16),
            pltpu.VMEM((sides, rows, 128), F32),
            pltpu.VMEM((sides, rows, 128), F32),
            pltpu.VMEM((sides * rows, 128), I32),
            pltpu.VMEM(density.shape, F32),
            pltpu.VMEM(density.shape, F32),
            pltpu.VMEM((hidden, width), BF16),
            pltpu.VMEM((levels, hidden, hidden), BF16),
            pltpu.VMEM((levels + 1, hidden, 128), F32),
            dma((sides,)), dma((sides,)), dma((sides,)), dma((sides,)), dma((8,)), dma((8,)), dma,
        ],
        compiler_params=pltpu.CompilerParams(
            collective_id=0, has_side_effects=True, vmem_limit_bytes=48 << 20
        ),
        name="blend",
    )(
        density, feat, band_cell[0, 0], band_count[0, 0], w_in[0, 0], w_hid[0, 0],
        w_out[0, 0][None, :], biases[0, 0],
    )
    return pl.pallas_call(
        finish_kernel,
        out_shape=(
            jax.ShapeDtypeStruct(density.shape, F32),
            jax.ShapeDtypeStruct((3,) + density.shape, F32),
        ),
        in_specs=[vmem],
        out_specs=(vmem, vmem),
        scratch_shapes=[pltpu.VMEM(full, F32), pltpu.VMEM(full, F32)],
        compiler_params=pltpu.CompilerParams(vmem_limit_bytes=32 << 20),
        name="finish",
    )(ext)


def solution(mesh):
    placed = (
        P("bx", "by", None),
        P("bx", "by", None, None, None),
        P("bx", "by", None, None),
        P("bx", "by", None),
        P("bx", "by", None, None),
        P("bx", "by", None, None, None),
        P("bx", "by", None),
        P("bx", "by", None, None),
    )
    return jax.shard_map(
        shards,
        mesh=mesh,
        in_specs=placed,
        out_specs=(P("bx", "by", None), P(None, "bx", "by", None)),
        check_vma=False,
    )
```

```python
import functools

import jax
import jax.numpy as jnp
from jax import lax
from jax.experimental import pallas as pl
from jax.experimental.pallas import tpu as pltpu
from jax.sharding import PartitionSpec as P

MESH = pl.DeviceIdType.MESH
F32, BF16, I32 = jnp.float32, jnp.bfloat16, jnp.int32
HX, HY = 4, 8
GROUP = 4
ROUTES = (2, 1, 2, 1)
ROW_PARTS = 1
AROUND = ((-1, 0), (1, 0), (0, -1), (0, 1), (-1, -1), (-1, 1), (1, -1), (1, 1))


def spread(row, index):
    wide = jnp.broadcast_to(row, index.shape)
    return jnp.take_along_axis(wide, index, axis=1, mode="promise_in_bounds")


def blend_kernel(
    dens, feat, cell, count, w_in, w_hid, w_out, bias, out,
    field, coef_x, coef_y, recv, cells, tile_lo, tile_hi, tiles_in, cells_in, table,
    nets, up, down, left, right, values_in, values,
    cell_v, count_s, win_v, whid_v, wout_v, bias_v, win_t, whid_t, bias_w,
    relayed, load_sem, far_send, far_recv, relay_send, relay_recv, feat_send, feat_recv, dens_send, dens_recv, cell_send, cell_recv, value_send, value_recv,
):
    ix, iy = lax.axis_index("bx"), lax.axis_index("by")
    nx, ny = lax.axis_size("bx"), lax.axis_size("by")
    size_x, size_y, size_z = dens.shape
    listed = cell.shape[1]
    rows = listed // 128
    wide = size_x + 2 * HX
    base_2, base_3 = wide, wide + wide // 2

    def there(dx, dy):
        ok_x = jnp.bool_(True) if dx == 0 else (ix + dx >= 0 if dx < 0 else ix + dx < nx)
        ok_y = jnp.bool_(True) if dy == 0 else (iy + dy >= 0 if dy < 0 else iy + dy < ny)
        return ok_x & ok_y

    def at(dx, dy):
        return {"bx": ix + dx, "by": iy + dy}

    loads = [
        pltpu.make_async_copy(src, dst, load_sem.at[n])
        for n, (src, dst) in enumerate(
            ((cell, cell_v), (count, count_s), (w_hid, whid_v), (w_in, win_v), (w_out, wout_v), (bias, bias_v),
             (dens, field.at[pl.ds(HX, size_x), pl.ds(HY, size_y), :]))
        )
    ]
    field[0:HX] = jnp.zeros_like(field[0:HX])
    field[HX + size_x :] = jnp.zeros_like(field[HX + size_x :])
    field[HX : HX + size_x, 0:HY, :] = jnp.zeros((size_x, HY, size_z), F32)
    field[HX : HX + size_x, HY + size_y :, :] = jnp.zeros((size_x, HY, size_z), F32)
    values_in[...] = jnp.zeros_like(values_in)
    nets[...] = jnp.zeros_like(nets)
    tiles_in[...] = jnp.full_like(tiles_in, -1)
    cells_in[...] = jnp.full_like(cells_in, -1)
    for load in loads:
        load.start()
    place_in = ix % GROUP
    flows = []
    for step, first in ((1, GROUP - 1), (-1, 0)):
        def starts(shift, step=step, first=first):
            origin = ix + shift
            return (origin % GROUP == first) & (origin >= 0) & (origin < nx) & (origin + step >= 0) & (origin + step < nx)

        flows.append((step, 1 if step > 0 else 0, starts))
    behind = sorted({r for r in ROUTES if r})
    expected = sum(there(dx, dy).astype(I32) for dx, dy in AROUND)
    barrier = pltpu.get_barrier_semaphore()
    for dx, dy in AROUND:
        @pl.when(there(dx, dy))
        def _(dx=dx, dy=dy):
            pl.semaphore_signal(barrier, inc=1, device_id=at(dx, dy), device_id_type=MESH)

    for step, _side, starts in flows:
        for r in behind:
            if r > 1:
                @pl.when(starts(r * step))
                def _(r=r, step=step):
                    pl.semaphore_signal(barrier, inc=1, device_id=at(r * step, 0), device_id_type=MESH)

                expected = expected + starts(0).astype(I32)

            @pl.when(starts(-step))
            def _(r=r, step=step):
                pl.semaphore_signal(barrier, inc=1, device_id=at(-(r + 1) * step, 0), device_id_type=MESH)

            expected = expected + starts(r * step).astype(I32)

    loads[0].wait()
    loads[1].wait()
    ranks = lax.broadcasted_iota(I32, (1, listed), 1)
    for s in range(4):
        usable = (ranks < count_s[0, s]) & there(*AROUND[s])
        height = jnp.where(usable, cell_v[s : s + 1, :] & (size_z - 1), -1)
        for r in range(rows):
            cells[s * rows + r : s * rows + r + 1, :] = height[:, r * 128 : (r + 1) * 128]
    pairs = HX // 2
    tile_lo[0:HX] = cells[0:HX]
    tile_hi[0:HX] = cells[2 * rows - HX : 2 * rows]
    for n, s in enumerate((2, 3)):
        tile_lo[HX + n * pairs : HX + (n + 1) * pairs] = cells[s * rows : s * rows + pairs]
        tile_hi[HX + n * pairs : HX + (n + 1) * pairs] = cells[(s + 1) * rows - pairs : (s + 1) * rows]

    def fill(which, source):
        table[which, HX : HX + size_x] = source[0 : 2 * rows]
        for n, base in enumerate((base_2, base_3)):
            table[which, base + pairs : base + pairs + rows] = source[(2 + n) * rows : (3 + n) * rows]

    def fill_strips(which, lo, hi):
        table[which, 0:HX] = lo[0:HX]
        table[which, HX + size_x : wide] = hi[0:HX]
        for n, base in enumerate((base_2, base_3)):
            table[which, base : base + pairs] = lo[HX + n * pairs : HX + (n + 1) * pairs]
            table[which, base + pairs + rows : base + rows + 2 * pairs] = hi[HX + n * pairs : HX + (n + 1) * pairs]

    lane = lax.broadcasted_iota(I32, (8, 128), 1)
    sub = lax.broadcasted_iota(I32, (8, 128), 0)
    groups = size_y // 8
    half = groups // 2
    index = [4 * (8 * g + sub) + lane // 32 for g in range(groups)]
    dist_y = [((8 * g + sub).astype(F32) + 0.5) / size_y - 0.5 for g in range(groups)]
    own_groups = [(0, g, HY + 8 * g) for g in range(groups)]
    side_groups = [(1, groups - 1, 0), (2, 0, HY + size_y)]

    def entries(lists, which, g, pair, parity):
        row_x = lists[which, pl.ds(2 * pair + parity, 1), :]
        row_y = lists[which, pl.ds((base_2 if g < half else base_3) + pair, 1), :]
        return spread(row_x, index[g]), spread(row_y, index[g % half + half * parity])

    def prepare(chosen):
        def step(pair, _):
            for parity in range(2):
                x = 2 * pair + parity
                local = (x + size_x - HX) % size_x
                dist_x = (local.astype(F32) + 0.5) / size_x - 0.5
                off_x = jnp.where(local < size_x // 2, -1.0, 1.0)
                for which, g, place in chosen:
                    in_x, in_y = entries(table, which, g, pair, parity)
                    off_y = -1.0 if g < half else 1.0
                    sq_x, sq_y = dist_x * dist_x, dist_y[g] * dist_y[g]
                    far_x, far_y = dist_x - off_x, dist_y[g] - off_y
                    own = 1.0 / (sq_x + sq_y + 0.25)
                    w_x = jnp.where(in_x == lane, 1.0 / (far_x * far_x + sq_y + 0.25), 0.0)
                    w_y = jnp.where(in_y == lane, 1.0 / (sq_x + far_y * far_y + 0.25), 0.0)
                    share = 1.0 / (own + w_x + w_y)
                    voxels = pl.ds(place, 8)
                    field[x, voxels, :] = own * field[x, voxels, :] * share
                    coef_x[x, voxels, :] = w_x * share
                    coef_y[x, voxels, :] = w_y * share
            return 0

        return step

    fill(0, cells)
    for load in loads[2:]:
        load.wait()
    lax.fori_loop(pairs, wide // 2 - pairs, prepare(own_groups), 0)
    for layer in range(w_hid.shape[0]):
        whid_t[layer] = whid_v[layer].T
    win_t[...] = win_v[...].T
    for layer in range(bias.shape[0]):
        bias_w[layer] = jnp.broadcast_to(bias_v[layer], (128, bias.shape[2])).T

    pl.semaphore_wait(barrier, expected)

    def remote(src, dst, send, arrive, n, dx, dy):
        return pltpu.make_async_remote_copy(
            src_ref=src, dst_ref=dst, send_sem=send.at[n], recv_sem=arrive.at[n],
            device_id=at(dx, dy), device_id_type=MESH)

    def opposite(s):
        dx = jnp.where(s == 0, 1, jnp.where(s == 1, -1, 0))
        dy = jnp.where(s == 2, 1, jnp.where(s == 3, -1, 0))
        ok = (ix + dx >= 0) & (ix + dx < nx) & (iy + dy >= 0) & (iy + dy < ny)
        return ok, dx, dy

    def feature_copy(s, dx, dy):
        return remote(feat.at[s], recv.at[s], feat_send, feat_recv, s, dx, dy)

    def cut(d, own, width, inner):
        if d == 0:
            return pl.ds(0, inner), pl.ds(own, inner)
        if d > 0:
            return pl.ds(inner - width, width), pl.ds(own - width, width)
        return pl.ds(0, width), pl.ds(own + inner, width)

    def density_copy(n, dx, dy):
        src_x, dst_x = cut(dx, HX, HX, size_x)
        src_y, dst_y = cut(dy, HY, HY, size_y)
        return remote(
            dens.at[src_x, src_y, :], field.at[dst_x, dst_y, :], dens_send, dens_recv, n, dx, dy
        )

    def cell_copy(n, dx, dy):
        m = AROUND.index((-dx, -dy))
        if dx == 0:
            return remote(cells, cells_in.at[m - 2], cell_send, cell_recv, n, dx, dy)
        return remote(tile_lo if dx < 0 else tile_hi, tiles_in.at[m], cell_send, cell_recv, n, dx, dy)

    def value_copy(n, dx, dy):
        m = AROUND.index((-dx, -dy))
        src = (left if dy < 0 else right) if dx == 0 else (down if dx < 0 else up)
        return remote(src, values_in.at[m], value_send, value_recv, n, dx, dy)

    part_rows = feat.shape[1] // ROW_PARTS
    part_columns = listed * ROW_PARTS // len(ROUTES)

    def piece(ref, s, n):
        return ref.at[
            s, pl.ds(n % ROW_PARTS * part_rows, part_rows), pl.ds(n // ROW_PARTS * part_columns, part_columns)
        ]

    def far_copy(n, side, step):
        r = ROUTES[n]
        if r:
            dst, arrive, shift = relayed.at[side, n], relay_recv.at[side, n], -r * step
        else:
            dst, arrive, shift = piece(recv, side, n), far_recv.at[n], step
        return pltpu.make_async_remote_copy(
            src_ref=piece(feat, side, n), dst_ref=dst, send_sem=far_send.at[n], recv_sem=arrive,
            device_id=at(shift, 0), device_id_type=MESH)

    def forward_copy(n, side, step):
        return pltpu.make_async_remote_copy(
            src_ref=relayed.at[side, n], dst_ref=piece(recv, side, n), send_sem=relay_send.at[side, n],
            recv_sem=far_recv.at[n], device_id=at((ROUTES[n] + 1) * step, 0), device_id_type=MESH)

    for step, side, starts in flows:
        @pl.when(starts(0))
        def _(step=step, side=side):
            for n in range(len(ROUTES)):
                far_copy(n, side, step).start()

    def near(s):
        ok = there(*AROUND[s])
        for step, side, starts in flows:
            if s == side:
                ok = ok & jnp.logical_not(starts(0))
        return ok

    for s in (2, 3, 0, 1):
        @pl.when(near(s))
        def _(s=s):
            feature_copy(s, *AROUND[s]).start()

    for n in range(len(ROUTES)):
        for step, side, starts in flows:
            if ROUTES[n]:
                @pl.when(starts(ROUTES[n] * step))
                def _(n=n, step=step, side=side):
                    far_copy(n, side, step).wait_recv()
                    forward_copy(n, side, step).start()

    for n, (dx, dy) in enumerate(AROUND):
        @pl.when(there(dx, dy))
        def _(n=n, dx=dx, dy=dy):
            cell_copy(n, dx, dy).start()
            density_copy(n, dx, dy).start()

    head = jnp.broadcast_to(wout_v[...].astype(F32), (16, w_out.shape[1])).astype(BF16)
    last = ix % 4 == 3

    def evaluate(step, _):
        s = jnp.where(step < 2, step + 2, jnp.where(last, 3 - step, step - 2))
        ok, dx, dy = opposite(s)

        @pl.when(ok)
        def _():
            far = ((s == 1) & flows[0][2](-1)) | ((s == 0) & flows[1][2](1))

            @pl.when(far)
            def _():
                for n in range(len(ROUTES)):
                    pltpu.make_async_remote_copy(
                        src_ref=piece(recv, s, n), dst_ref=piece(recv, s, n), send_sem=far_send.at[n],
                        recv_sem=far_recv.at[n], device_id=at(dx, dy), device_id_type=MESH).wait_recv()

            @pl.when(jnp.logical_not(far))
            def _():
                feature_copy(s, dx, dy).wait_recv()

            def layer(weights, hidden, level):
                column = jnp.concatenate([bias_w[level]] * (listed // 128), axis=1)
                total = jnp.dot(weights, hidden, preferred_element_type=F32) + column
                return jnp.maximum(total.astype(BF16), 0)

            hidden = layer(win_t[...], recv[s], 0)
            for level in range(whid_t.shape[0]):
                hidden = layer(whid_t[level], hidden, level + 1)
            raw = jnp.dot(head, hidden, preferred_element_type=F32)[0:1, :]
            result = jnp.maximum(raw, 0.0) + jnp.log1p(jnp.exp(-jnp.abs(raw)))
            for r in range(rows):
                nets[s, r : r + 1, :] = result[:, r * 128 : (r + 1) * 128]

        return 0

    lax.fori_loop(0, 4, evaluate, 0)

    up[0:rows] = nets[0]
    down[0:rows] = nets[1]
    left[0:rows] = nets[3]
    right[0:rows] = nets[2]
    for n, s in enumerate((2, 3)):
        up[rows + n * pairs : rows + (n + 1) * pairs] = nets[s, rows - pairs : rows]
        down[rows + n * pairs : rows + (n + 1) * pairs] = nets[s, 0:pairs]
    for side in (left, right):
        side[rows : rows + HX] = nets[0, 0:HX]
        side[rows + HX : rows + 2 * HX] = nets[1, rows - HX : rows]
    for n, (dx, dy) in enumerate(AROUND):
        @pl.when(there(dx, dy))
        def _(n=n, dx=dx, dy=dy):
            value_copy(n, dx, dy).start()

    for n, (dx, dy) in enumerate(AROUND):
        @pl.when(there(-dx, -dy))
        def _(n=n, dx=dx, dy=dy):
            cell_copy(n, dx, dy).wait_recv()
            density_copy(n, dx, dy).wait_recv()

    fill(1, cells_in.at[0])
    fill(2, cells_in.at[1])
    fill_strips(0, tiles_in.at[0], tiles_in.at[1])
    fill_strips(1, tiles_in.at[4], tiles_in.at[6])
    fill_strips(2, tiles_in.at[5], tiles_in.at[7])
    lax.fori_loop(0, pairs, prepare(own_groups), 0)
    lax.fori_loop(wide // 2 - pairs, wide // 2, prepare(own_groups), 0)
    lax.fori_loop(0, wide // 2, prepare(side_groups), 0)

    for n, (dx, dy) in enumerate(AROUND):
        @pl.when(there(-dx, -dy))
        def _(n=n, dx=dx, dy=dy):
            value_copy(n, dx, dy).wait_recv()

    def put(which, first, source):
        values[which, first : first + source.shape[0]] = source

    tail, strip = HX + size_x, rows
    lo_2, hi_2 = base_2 + pairs, base_2 + pairs + rows
    lo_3, hi_3 = base_3 + pairs, base_3 + pairs + rows
    west, east, south, north = (values_in.at[m] for m in range(4))
    south_west, north_west, south_east, north_east = (values_in.at[m] for m in range(4, 8))
    put(0, HX, west[0:rows])
    put(0, HX + rows, east[0:rows])
    put(0, 0, nets[1, rows - HX : rows])
    put(0, tail, nets[0, 0:HX])
    put(0, lo_2, south[0:rows])
    put(0, lo_3, north[0:rows])
    put(0, base_2, south_west[strip : strip + pairs])
    put(0, base_3, north_west[strip + pairs : strip + 2 * pairs])
    put(0, hi_2, south_east[strip : strip + pairs])
    put(0, hi_3, north_east[strip + pairs : strip + 2 * pairs])
    for which, column, to_west, to_east in ((1, south, south_west, south_east), (2, north, north_west, north_east)):
        put(which, HX, to_west[0:rows])
        put(which, HX + rows, to_east[0:rows])
        put(which, 0, column[strip + HX : strip + 2 * HX])
        put(which, tail, column[strip : strip + HX])
    put(1, lo_3, nets[3])
    put(1, base_3, west[strip + pairs : strip + 2 * pairs])
    put(1, hi_3, east[strip + pairs : strip + 2 * pairs])
    put(2, lo_2, nets[2])
    put(2, base_2, west[strip : strip + pairs])
    put(2, hi_2, east[strip : strip + pairs])

    def blend(pair, _):
        for parity in range(2):
            x = 2 * pair + parity
            for which, g, place in own_groups + side_groups:
                from_x, from_y = entries(values, which, g, pair, parity)
                voxels = pl.ds(place, 8)
                out[x, voxels, :] = (
                    field[x, voxels, :] + coef_x[x, voxels, :] * from_x + coef_y[x, voxels, :] * from_y
                )
        return 0

    lax.fori_loop(0, wide // 2, blend, 0)

    for s in range(4):
        @pl.when(near(s))
        def _(s=s):
            feature_copy(s, *AROUND[s]).wait_send()

    for step, side, starts in flows:
        @pl.when(starts(0))
        def _(step=step, side=side):
            for n in range(len(ROUTES)):
                far_copy(n, side, step).wait_send()

        for n in range(len(ROUTES)):
            if ROUTES[n]:
                @pl.when(starts(ROUTES[n] * step))
                def _(n=n, step=step, side=side):
                    forward_copy(n, side, step).wait_send()

    for n, (dx, dy) in enumerate(AROUND):
        @pl.when(there(dx, dy))
        def _(n=n, dx=dx, dy=dy):
            cell_copy(n, dx, dy).wait_send()
            density_copy(n, dx, dy).wait_send()
            value_copy(n, dx, dy).wait_send()


def finish_kernel(ext, smoothed, normals, one, two):
    ix, iy = lax.axis_index("bx"), lax.axis_index("by")
    nx, ny = lax.axis_size("bx"), lax.axis_size("by")
    size_x, size_y, size_z = smoothed.shape
    full_x, full_y = size_x + 2 * HX, size_y + 2 * HY
    sub = lax.broadcasted_iota(I32, (full_y, size_z), 0)
    inside_y = ((sub >= HY) | (iy > 0)) & ((sub < HY + size_y) | (iy < ny - 1))
    keep_y = jnp.where(inside_y, 0.2, 0.0)

    def one_pass(src, dst, margin):
        def step(x, _):
            centre = src[x]
            total = (
                centre + src[x + 1] + src[x - 1]
                + pltpu.roll(centre, 1, 0) + pltpu.roll(centre, full_y - 1, 0)
            )
            inside = ((x >= HX) | (ix > 0)) & ((x < HX + size_x) | (ix < nx - 1))
            dst[x] = total * jnp.where(inside, keep_y, 0.0)
            return 0

        lax.fori_loop(margin, full_x - margin, step, 0, unroll=2)

    one_pass(ext, one, 1)
    one_pass(one, two, 2)
    one_pass(two, one, 3)
    last_z = lax.broadcasted_iota(I32, (size_y, size_z), 1)

    def gradient(x, _):
        row = HX + x
        centre = one[row]
        own = centre[HY : HY + size_y]
        grad_x = one[row + 1, HY : HY + size_y, :] - one[row - 1, HY : HY + size_y, :]
        grad_y = (pltpu.roll(centre, full_y - 1, 0) - pltpu.roll(centre, 1, 0))[HY : HY + size_y]
        after = jnp.where(last_z == size_z - 1, 0.0, pltpu.roll(own, size_z - 1, 1))
        before = jnp.where(last_z == 0, 0.0, pltpu.roll(own, 1, 1))
        grad_z = after - before
        factor = lax.rsqrt(1.0 + grad_x * grad_x + grad_y * grad_y + grad_z * grad_z)
        smoothed[x] = own
        normals[0, x] = grad_x * factor
        normals[1, x] = grad_y * factor
        normals[2, x] = grad_z * factor
        return 0

    lax.fori_loop(0, size_x, gradient, 0, unroll=2)


def shards(density, band_feat, band_cell, band_count, w_in, w_hid, w_out, biases):
    size_x, size_y, size_z = density.shape
    feat = jnp.swapaxes(band_feat[0, 0], 1, 2)
    sides, width, listed = feat.shape
    levels, hidden = w_hid.shape[2], w_hid.shape[3]
    rows = listed // 128
    full = (size_x + 2 * HX, size_y + 2 * HY, size_z)
    vmem = pl.BlockSpec(memory_space=pltpu.VMEM)
    hbm = pl.BlockSpec(memory_space=pltpu.HBM)
    dma = pltpu.SemaphoreType.DMA
    own_cells = (sides * rows, 128)
    message = (rows + 2 * HX, 128)
    tables = (3, 2 * full[0], 128)
    ext = pl.pallas_call(
        blend_kernel,
        out_shape=jax.ShapeDtypeStruct(full, F32),
        in_specs=[hbm] * 8,
        out_specs=vmem,
        scratch_shapes=[
            pltpu.VMEM(full, F32),
            pltpu.VMEM(full, F32),
            pltpu.VMEM(full, F32),
            pltpu.VMEM((sides, width, listed), BF16),
            pltpu.VMEM(own_cells, I32),
            pltpu.VMEM((2 * HX, 128), I32),
            pltpu.VMEM((2 * HX, 128), I32),
            pltpu.VMEM((8, 2 * HX, 128), I32),
            pltpu.VMEM((2,) + own_cells, I32),
            pltpu.VMEM(tables, I32),
            pltpu.VMEM((sides, rows, 128), F32),
            pltpu.VMEM(message, F32),
            pltpu.VMEM(message, F32),
            pltpu.VMEM(message, F32),
            pltpu.VMEM(message, F32),
            pltpu.VMEM((8,) + message, F32),
            pltpu.VMEM(tables, F32),
            pltpu.VMEM((sides, listed), I32),
            pltpu.SMEM((1, sides), I32),
            pltpu.VMEM((width, hidden), BF16),
            pltpu.VMEM((levels, hidden, hidden), BF16),
            pltpu.VMEM((1, hidden), BF16),
            pltpu.VMEM((levels + 1, 1, hidden), F32),
            pltpu.VMEM((hidden, width), BF16),
            pltpu.VMEM((levels, hidden, hidden), BF16),
            pltpu.VMEM((levels + 1, hidden, 128), F32),
            pltpu.VMEM((2, len(ROUTES), width // ROW_PARTS, listed * ROW_PARTS // len(ROUTES)), BF16),
            dma((7,)), dma((len(ROUTES),)), dma((len(ROUTES),)), dma((2, len(ROUTES))), dma((2, len(ROUTES))),
            dma((sides,)), dma((sides,)),
            dma((8,)), dma((8,)), dma((8,)), dma((8,)), dma((8,)), dma((8,)),
        ],
        compiler_params=pltpu.CompilerParams(
            collective_id=0, has_side_effects=True, vmem_limit_bytes=61 << 20
        ),
        name="blend",
    )(
        density, feat, band_cell[0, 0], band_count[0], w_in[0, 0], w_hid[0, 0],
        w_out[0], biases[0, 0][:, None, :],
    )
    return pl.pallas_call(
        finish_kernel,
        out_shape=(
            jax.ShapeDtypeStruct(density.shape, F32),
            jax.ShapeDtypeStruct((3,) + density.shape, F32),
        ),
        in_specs=[vmem],
        out_specs=(vmem, vmem),
        scratch_shapes=[pltpu.VMEM(full, F32), pltpu.VMEM(full, F32)],
        compiler_params=pltpu.CompilerParams(vmem_limit_bytes=32 << 20),
        name="finish",
    )(ext)


def solution(mesh):
    placed = (
        P("bx", "by", None),
        P("bx", "by", None, None, None),
        P("bx", "by", None, None),
        P("bx", "by", None),
        P("bx", "by", None, None),
        P("bx", "by", None, None, None),
        P("bx", "by", None),
        P("bx", "by", None, None),
    )
    return jax.shard_map(
        shards,
        mesh=mesh,
        in_specs=placed,
        out_specs=(P("bx", "by", None), P(None, "bx", "by", None)),
        check_vma=False,
    )
```

```python
import functools

import jax
import jax.numpy as jnp
from jax import lax
from jax.experimental import pallas as pl
from jax.experimental.pallas import tpu as pltpu
from jax.sharding import PartitionSpec as P

MESH = pl.DeviceIdType.MESH
F32, BF16, I32 = jnp.float32, jnp.bfloat16, jnp.int32
HX, HY = 4, 8
GROUP = 4
ROUTES = (2, 1, 2, 1, 0, 2, 1, 2)
ROW_PARTS = 2
AROUND = ((-1, 0), (1, 0), (0, -1), (0, 1), (-1, -1), (-1, 1), (1, -1), (1, 1))


def spread(row, index):
    wide = jnp.broadcast_to(row, index.shape)
    return jnp.take_along_axis(wide, index, axis=1, mode="promise_in_bounds")


def blend_kernel(
    dens, feat, cell, count, w_in, w_hid, w_out, bias, out,
    field, side_after, side_before, coef_x, coef_y, recv, cells, tile_lo, tile_hi, tiles_in, cells_in, table,
    nets, up, down, left, right, values_in, values,
    cell_v, count_s, win_v, whid_v, wout_v, bias_v, win_t, whid_t, bias_w,
    relayed, load_sem, far_send, far_recv, relay_send, relay_recv, feat_send, feat_recv, dens_send, dens_recv, cell_send, cell_recv, value_send, value_recv, out_sem,
):
    ix, iy = lax.axis_index("bx"), lax.axis_index("by")
    nx, ny = lax.axis_size("bx"), lax.axis_size("by")
    size_x, size_y, size_z = dens.shape
    listed = cell.shape[1]
    rows = listed // 128
    wide = size_x + 2 * HX
    base_2, base_3 = wide, wide + wide // 2

    def there(dx, dy):
        ok_x = jnp.bool_(True) if dx == 0 else (ix + dx >= 0 if dx < 0 else ix + dx < nx)
        ok_y = jnp.bool_(True) if dy == 0 else (iy + dy >= 0 if dy < 0 else iy + dy < ny)
        return ok_x & ok_y

    def at(dx, dy):
        return {"bx": ix + dx, "by": iy + dy}

    loads = [
        pltpu.make_async_copy(src, dst, load_sem.at[n])
        for n, (src, dst) in enumerate(
            ((cell, cell_v), (count, count_s), (w_hid, whid_v), (w_in, win_v), (w_out, wout_v), (bias, bias_v),
             (dens, field.at[pl.ds(HX, size_x), pl.ds(0, size_y), :]))
        )
    ]
    field[0:HX] = jnp.zeros_like(field[0:HX])
    field[HX + size_x :] = jnp.zeros_like(field[HX + size_x :])
    side_after[...] = jnp.zeros_like(side_after)
    side_before[...] = jnp.zeros_like(side_before)
    values_in[...] = jnp.zeros_like(values_in)
    nets[...] = jnp.zeros_like(nets)
    tiles_in[...] = jnp.full_like(tiles_in, -1)
    cells_in[...] = jnp.full_like(cells_in, -1)
    for load in loads:
        load.start()
    place_in = ix % GROUP
    flows = []
    for step, first in ((1, GROUP - 1), (-1, 0)):
        def starts(shift, step=step, first=first):
            origin = ix + shift
            return (origin % GROUP == first) & (origin >= 0) & (origin < nx) & (origin + step >= 0) & (origin + step < nx)

        flows.append((step, 1 if step > 0 else 0, starts))
    behind = sorted({r for r in ROUTES if r})
    expected = sum(there(dx, dy).astype(I32) for dx, dy in AROUND)
    barrier = pltpu.get_barrier_semaphore()
    for dx, dy in AROUND:
        @pl.when(there(dx, dy))
        def _(dx=dx, dy=dy):
            pl.semaphore_signal(barrier, inc=1, device_id=at(dx, dy), device_id_type=MESH)

    for step, _side, starts in flows:
        for r in behind:
            if r > 1:
                @pl.when(starts(r * step))
                def _(r=r, step=step):
                    pl.semaphore_signal(barrier, inc=1, device_id=at(r * step, 0), device_id_type=MESH)

                expected = expected + starts(0).astype(I32)

            @pl.when(starts(-step))
            def _(r=r, step=step):
                pl.semaphore_signal(barrier, inc=1, device_id=at(-(r + 1) * step, 0), device_id_type=MESH)

            expected = expected + starts(r * step).astype(I32)

    loads[0].wait()
    loads[1].wait()
    ranks = lax.broadcasted_iota(I32, (1, listed), 1)
    for s in range(4):
        usable = (ranks < count_s[0, s]) & there(*AROUND[s])
        height = jnp.where(usable, cell_v[s : s + 1, :] & (size_z - 1), -1)
        for r in range(rows):
            cells[s * rows + r : s * rows + r + 1, :] = height[:, r * 128 : (r + 1) * 128]
    pairs = HX // 2
    tile_lo[0:HX] = cells[0:HX]
    tile_hi[0:HX] = cells[2 * rows - HX : 2 * rows]
    for n, s in enumerate((2, 3)):
        tile_lo[HX + n * pairs : HX + (n + 1) * pairs] = cells[s * rows : s * rows + pairs]
        tile_hi[HX + n * pairs : HX + (n + 1) * pairs] = cells[(s + 1) * rows - pairs : (s + 1) * rows]

    def fill(which, source):
        table[which, HX : HX + size_x] = source[0 : 2 * rows]
        for n, base in enumerate((base_2, base_3)):
            table[which, base + pairs : base + pairs + rows] = source[(2 + n) * rows : (3 + n) * rows]

    def fill_strips(which, lo, hi):
        table[which, 0:HX] = lo[0:HX]
        table[which, HX + size_x : wide] = hi[0:HX]
        for n, base in enumerate((base_2, base_3)):
            table[which, base : base + pairs] = lo[HX + n * pairs : HX + (n + 1) * pairs]
            table[which, base + pairs + rows : base + rows + 2 * pairs] = hi[HX + n * pairs : HX + (n + 1) * pairs]

    lane = lax.broadcasted_iota(I32, (8, 128), 1)
    sub = lax.broadcasted_iota(I32, (8, 128), 0)
    groups = size_y // 8
    half = groups // 2
    index = [4 * (8 * g + sub) + lane // 32 for g in range(groups)]
    dist_y = [((8 * g + sub).astype(F32) + 0.5) / size_y - 0.5 for g in range(groups)]
    after = sub < HX

    def both(first, second):
        return jnp.where(after, first, second)

    top = groups - 1
    index_side = both(index[0], index[top])
    index_side_y = [both(index[half * parity], index[top % half + half * parity]) for parity in range(2)]
    dist_side, off_side = both(dist_y[0], dist_y[top]), both(-1.0, 1.0)

    def entries(lists, g, pair, parity):
        def row(which, at_row):
            return lists[which, pl.ds(at_row, 1), :]

        x = 2 * pair + parity
        if g < groups:
            row_y = row(0, (base_2 if g < half else base_3) + pair)
            return spread(row(0, x), index[g]), spread(row_y, index[g % half + half * parity])
        row_x = both(row(2, x), row(1, x))
        row_y = both(row(2, base_2 + pair), row(1, base_3 + pair))
        return spread(row_x, index_side), spread(row_y, index_side_y[parity])

    def prepare(chosen):
        def step(pair, _):
            for parity in range(2):
                x = 2 * pair + parity
                local = (x + size_x - HX) % size_x
                dist_x = (local.astype(F32) + 0.5) / size_x - 0.5
                off_x = jnp.where(local < size_x // 2, -1.0, 1.0)
                for g in chosen:
                    in_x, in_y = entries(table, g, pair, parity)
                    voxels = pl.ds(8 * g, 8)
                    if g < groups:
                        across, off_y = dist_y[g], -1.0 if g < half else 1.0
                        density = field[x, voxels, :]
                    else:
                        across, off_y = dist_side, off_side
                        density = both(side_after[x], side_before[x])
                    sq_x, sq_y = dist_x * dist_x, across * across
                    far_x, far_y = dist_x - off_x, across - off_y
                    own = 1.0 / (sq_x + sq_y + 0.25)
                    w_x = jnp.where(in_x == lane, 1.0 / (far_x * far_x + sq_y + 0.25), 0.0)
                    w_y = jnp.where(in_y == lane, 1.0 / (sq_x + far_y * far_y + 0.25), 0.0)
                    share = 1.0 / (own + w_x + w_y)
                    field[x, voxels, :] = own * density * share
                    coef_x[x, voxels, :] = w_x * share
                    coef_y[x, voxels, :] = w_y * share
            return 0

        return step

    own_groups = tuple(range(groups))
    fill(0, cells)
    for load in loads[2:]:
        load.wait()
    lax.fori_loop(pairs, wide // 2 - pairs, prepare(own_groups), 0)
    for layer in range(w_hid.shape[0]):
        whid_t[layer] = whid_v[layer].T
    win_t[...] = win_v[...].T
    for layer in range(bias.shape[0]):
        bias_w[layer] = jnp.broadcast_to(bias_v[layer], (128, bias.shape[2])).T

    pl.semaphore_wait(barrier, expected)

    def remote(src, dst, send, arrive, n, dx, dy):
        return pltpu.make_async_remote_copy(
            src_ref=src, dst_ref=dst, send_sem=send.at[n], recv_sem=arrive.at[n],
            device_id=at(dx, dy), device_id_type=MESH)

    def opposite(s):
        dx = jnp.where(s == 0, 1, jnp.where(s == 1, -1, 0))
        dy = jnp.where(s == 2, 1, jnp.where(s == 3, -1, 0))
        ok = (ix + dx >= 0) & (ix + dx < nx) & (iy + dy >= 0) & (iy + dy < ny)
        return ok, dx, dy

    def feature_copy(s, dx, dy):
        return remote(feat.at[s], recv.at[s], feat_send, feat_recv, s, dx, dy)

    def density_copy(n, dx, dy):
        if dx == 0:
            src_x, dst_x = pl.ds(0, size_x), pl.ds(HX, size_x)
        elif dx > 0:
            src_x, dst_x = pl.ds(size_x - HX, HX), pl.ds(0, HX)
        else:
            src_x, dst_x = pl.ds(0, HX), pl.ds(HX + size_x, HX)
        if dy == 0:
            src, dst = dens.at[src_x], field.at[dst_x, pl.ds(0, size_y), :]
        elif dy > 0:
            src, dst = dens.at[src_x, pl.ds(size_y - HY, HY), :], side_before.at[dst_x]
        else:
            src, dst = dens.at[src_x, pl.ds(0, HY), :], side_after.at[dst_x]
        return remote(src, dst, dens_send, dens_recv, n, dx, dy)

    def cell_copy(n, dx, dy):
        m = AROUND.index((-dx, -dy))
        if dx == 0:
            return remote(cells, cells_in.at[m - 2], cell_send, cell_recv, n, dx, dy)
        return remote(tile_lo if dx < 0 else tile_hi, tiles_in.at[m], cell_send, cell_recv, n, dx, dy)

    def value_copy(n, dx, dy):
        m = AROUND.index((-dx, -dy))
        src = (left if dy < 0 else right) if dx == 0 else (down if dx < 0 else up)
        return remote(src, values_in.at[m], value_send, value_recv, n, dx, dy)

    part_rows = feat.shape[1] // ROW_PARTS
    part_columns = listed * ROW_PARTS // len(ROUTES)

    def piece(ref, s, n):
        return ref.at[
            s, pl.ds(n % ROW_PARTS * part_rows, part_rows), pl.ds(n // ROW_PARTS * part_columns, part_columns)
        ]

    def far_copy(n, side, step):
        r = ROUTES[n]
        if r:
            dst, arrive, shift = relayed.at[side, n], relay_recv.at[side, n], -r * step
        else:
            dst, arrive, shift = piece(recv, side, n), far_recv.at[n], step
        return pltpu.make_async_remote_copy(
            src_ref=piece(feat, side, n), dst_ref=dst, send_sem=far_send.at[n], recv_sem=arrive,
            device_id=at(shift, 0), device_id_type=MESH)

    def forward_copy(n, side, step):
        return pltpu.make_async_remote_copy(
            src_ref=relayed.at[side, n], dst_ref=piece(recv, side, n), send_sem=relay_send.at[side, n],
            recv_sem=far_recv.at[n], device_id=at((ROUTES[n] + 1) * step, 0), device_id_type=MESH)

    for step, side, starts in flows:
        @pl.when(starts(0))
        def _(step=step, side=side):
            for n in range(len(ROUTES)):
                far_copy(n, side, step).start()

    def near(s):
        ok = there(*AROUND[s])
        for step, side, starts in flows:
            if s == side:
                ok = ok & jnp.logical_not(starts(0))
        return ok

    for s in (2, 3, 0, 1):
        @pl.when(near(s))
        def _(s=s):
            feature_copy(s, *AROUND[s]).start()

    for step, side, starts in reversed(flows):
        for n in range(len(ROUTES)):
            if ROUTES[n]:
                @pl.when(starts(ROUTES[n] * step))
                def _(n=n, step=step, side=side):
                    far_copy(n, side, step).wait_recv()
                    forward_copy(n, side, step).start()

    for n, (dx, dy) in enumerate(AROUND):
        @pl.when(there(dx, dy))
        def _(n=n, dx=dx, dy=dy):
            cell_copy(n, dx, dy).start()
            density_copy(n, dx, dy).start()

    head = jnp.broadcast_to(wout_v[...].astype(F32), (16, w_out.shape[1])).astype(BF16)
    last = ix % 4 == 3

    def evaluate(step, _):
        s = jnp.where(step < 2, step + 2, jnp.where(last, 3 - step, step - 2))
        ok, dx, dy = opposite(s)

        @pl.when(ok)
        def _():
            far = ((s == 1) & flows[0][2](-1)) | ((s == 0) & flows[1][2](1))

            @pl.when(far)
            def _():
                for n in range(len(ROUTES)):
                    pltpu.make_async_remote_copy(
                        src_ref=piece(recv, s, n), dst_ref=piece(recv, s, n), send_sem=far_send.at[n],
                        recv_sem=far_recv.at[n], device_id=at(dx, dy), device_id_type=MESH).wait_recv()

            @pl.when(jnp.logical_not(far))
            def _():
                feature_copy(s, dx, dy).wait_recv()

            def layer(weights, hidden, level):
                column = jnp.concatenate([bias_w[level]] * (listed // 128), axis=1)
                total = jnp.dot(weights, hidden, preferred_element_type=F32) + column
                return jnp.maximum(total.astype(BF16), 0)

            hidden = layer(win_t[...], recv[s], 0)
            for level in range(whid_t.shape[0]):
                hidden = layer(whid_t[level], hidden, level + 1)
            raw = jnp.dot(head, hidden, preferred_element_type=F32)[0:1, :]
            result = jnp.maximum(raw, 0.0) + jnp.log1p(jnp.exp(-jnp.abs(raw)))
            for r in range(rows):
                nets[s, r : r + 1, :] = result[:, r * 128 : (r + 1) * 128]

        return 0

    lax.fori_loop(0, 4, evaluate, 0)

    up[0:rows] = nets[0]
    down[0:rows] = nets[1]
    left[0:rows] = nets[3]
    right[0:rows] = nets[2]
    for n, s in enumerate((2, 3)):
        up[rows + n * pairs : rows + (n + 1) * pairs] = nets[s, rows - pairs : rows]
        down[rows + n * pairs : rows + (n + 1) * pairs] = nets[s, 0:pairs]
    for side in (left, right):
        side[rows : rows + HX] = nets[0, 0:HX]
        side[rows + HX : rows + 2 * HX] = nets[1, rows - HX : rows]
    for n, (dx, dy) in enumerate(AROUND):
        @pl.when(there(dx, dy))
        def _(n=n, dx=dx, dy=dy):
            value_copy(n, dx, dy).start()

    for n, (dx, dy) in enumerate(AROUND):
        @pl.when(there(-dx, -dy))
        def _(n=n, dx=dx, dy=dy):
            cell_copy(n, dx, dy).wait_recv()
            density_copy(n, dx, dy).wait_recv()

    fill(1, cells_in.at[0])
    fill(2, cells_in.at[1])
    fill_strips(0, tiles_in.at[0], tiles_in.at[1])
    fill_strips(1, tiles_in.at[4], tiles_in.at[6])
    fill_strips(2, tiles_in.at[5], tiles_in.at[7])
    lax.fori_loop(0, pairs, prepare(own_groups), 0, unroll=True)
    lax.fori_loop(wide // 2 - pairs, wide // 2, prepare(own_groups), 0, unroll=True)
    lax.fori_loop(0, wide // 2, prepare((groups,)), 0, unroll=5)

    for n, (dx, dy) in enumerate(AROUND):
        @pl.when(there(-dx, -dy))
        def _(n=n, dx=dx, dy=dy):
            value_copy(n, dx, dy).wait_recv()

    def put(which, first, source):
        values[which, first : first + source.shape[0]] = source

    tail, strip = HX + size_x, rows
    lo_2, hi_2 = base_2 + pairs, base_2 + pairs + rows
    lo_3, hi_3 = base_3 + pairs, base_3 + pairs + rows
    west, east, south, north = (values_in.at[m] for m in range(4))
    south_west, north_west, south_east, north_east = (values_in.at[m] for m in range(4, 8))
    put(0, HX, west[0:rows])
    put(0, HX + rows, east[0:rows])
    put(0, 0, nets[1, rows - HX : rows])
    put(0, tail, nets[0, 0:HX])
    put(0, lo_2, south[0:rows])
    put(0, lo_3, north[0:rows])
    put(0, base_2, south_west[strip : strip + pairs])
    put(0, base_3, north_west[strip + pairs : strip + 2 * pairs])
    put(0, hi_2, south_east[strip : strip + pairs])
    put(0, hi_3, north_east[strip + pairs : strip + 2 * pairs])
    for which, column, to_west, to_east in ((1, south, south_west, south_east), (2, north, north_west, north_east)):
        put(which, HX, to_west[0:rows])
        put(which, HX + rows, to_east[0:rows])
        put(which, 0, column[strip + HX : strip + 2 * HX])
        put(which, tail, column[strip : strip + HX])
    put(1, lo_3, nets[3])
    put(1, base_3, west[strip + pairs : strip + 2 * pairs])
    put(1, hi_3, east[strip + pairs : strip + 2 * pairs])
    put(2, lo_2, nets[2])
    put(2, base_2, west[strip : strip + pairs])
    put(2, hi_2, east[strip : strip + pairs])

    def result_copy(chunk):
        part = pl.ds(8 * chunk, 8)
        return pltpu.make_async_copy(field.at[part], out.at[part], out_sem.at[chunk])

    def blend(chunk, _):
        for k in range(8):
            pair, parity = 4 * chunk + k // 2, k % 2
            x = 8 * chunk + k
            for g in range(groups + 1):
                from_x, from_y = entries(values, g, pair, parity)
                voxels = pl.ds(8 * g, 8)
                field[x, voxels, :] = (
                    field[x, voxels, :] + coef_x[x, voxels, :] * from_x + coef_y[x, voxels, :] * from_y
                )
        result_copy(chunk).start()
        return 0

    lax.fori_loop(0, wide // 8, blend, 0)

    for s in range(4):
        @pl.when(near(s))
        def _(s=s):
            feature_copy(s, *AROUND[s]).wait_send()

    for step, side, starts in flows:
        @pl.when(starts(0))
        def _(step=step, side=side):
            for n in range(len(ROUTES)):
                far_copy(n, side, step).wait_send()

        for n in range(len(ROUTES)):
            if ROUTES[n]:
                @pl.when(starts(ROUTES[n] * step))
                def _(n=n, step=step, side=side):
                    forward_copy(n, side, step).wait_send()

    for n, (dx, dy) in enumerate(AROUND):
        @pl.when(there(dx, dy))
        def _(n=n, dx=dx, dy=dy):
            cell_copy(n, dx, dy).wait_send()
            density_copy(n, dx, dy).wait_send()
            value_copy(n, dx, dy).wait_send()
    for chunk in range(wide // 8):
        result_copy(chunk).wait()


def finish_kernel(ext, smoothed, normals, zero, one, two, soft, grads, load_sem, soft_sem, grad_sem):
    ix, iy = lax.axis_index("bx"), lax.axis_index("by")
    nx, ny = lax.axis_size("bx"), lax.axis_size("by")
    size_x, size_y, size_z = smoothed.shape
    full_x, full_y = size_x + 2 * HX, size_y + HY
    chunks = full_x // 8

    def load(chunk):
        part = pl.ds(8 * chunk, 8)
        return pltpu.make_async_copy(ext.at[part], zero.at[part], load_sem.at[chunk])

    def store(chunk):
        part = pl.ds(8 * chunk, 8)
        return (
            pltpu.make_async_copy(soft.at[part], smoothed.at[part], soft_sem.at[chunk]),
            pltpu.make_async_copy(grads.at[:, part], normals.at[:, part], grad_sem.at[chunk]),
        )

    for chunk in range(chunks):
        load(chunk).start()
    sub = lax.broadcasted_iota(I32, (full_y, size_z), 0)
    inside_y = (sub < size_y) | ((sub < size_y + HX) & (iy < ny - 1)) | ((sub >= size_y + HX) & (iy > 0))
    keep_y = jnp.where(inside_y, 0.2, 0.0)

    def one_pass(src, dst, first, end):
        def step(x, _):
            centre = src[x]
            total = (
                centre + src[x + 1] + src[x - 1]
                + pltpu.roll(centre, 1, 0) + pltpu.roll(centre, full_y - 1, 0)
            )
            inside = ((x >= HX) | (ix > 0)) & ((x < HX + size_x) | (ix < nx - 1))
            dst[x] = total * jnp.where(inside, keep_y, 0.0)
            return 0

        lax.fori_loop(first, end, step, 0, unroll=4)

    for chunk in range(chunks):
        load(chunk).wait()
        one_pass(zero, one, max(1, 8 * chunk - 1), 8 * chunk + 7)
    one_pass(one, two, 2, full_x - 2)
    one_pass(two, one, 3, full_x - 3)
    last_z = lax.broadcasted_iota(I32, (size_y, size_z), 1)

    def gradient(chunk, _):
        for k in range(8):
            x = 8 * chunk + k
            row = HX + x
            centre = one[row]
            own = centre[0:size_y]
            grad_x = one[row + 1, 0:size_y, :] - one[row - 1, 0:size_y, :]
            grad_y = (pltpu.roll(centre, full_y - 1, 0) - pltpu.roll(centre, 1, 0))[0:size_y]
            ahead = jnp.where(last_z == size_z - 1, 0.0, pltpu.roll(own, size_z - 1, 1))
            behind = jnp.where(last_z == 0, 0.0, pltpu.roll(own, 1, 1))
            grad_z = ahead - behind
            factor = lax.rsqrt(1.0 + grad_x * grad_x + grad_y * grad_y + grad_z * grad_z)
            soft[x] = own
            grads[0, x] = grad_x * factor
            grads[1, x] = grad_y * factor
            grads[2, x] = grad_z * factor
        for copy in store(chunk):
            copy.start()
        return 0

    lax.fori_loop(0, size_x // 8, gradient, 0)
    for chunk in range(size_x // 8):
        for copy in store(chunk):
            copy.wait()


def shards(density, band_feat, band_cell, band_count, w_in, w_hid, w_out, biases):
    size_x, size_y, size_z = density.shape
    feat = jnp.swapaxes(band_feat[0, 0], 1, 2)
    sides, width, listed = feat.shape
    levels, hidden = w_hid.shape[2], w_hid.shape[3]
    rows = listed // 128
    full = (size_x + 2 * HX, size_y + HY, size_z)
    beside = (size_x + 2 * HX, HY, size_z)
    hbm = pl.BlockSpec(memory_space=pltpu.HBM)
    dma = pltpu.SemaphoreType.DMA
    own_cells = (sides * rows, 128)
    message = (rows + 2 * HX, 128)
    tables = (3, 2 * full[0], 128)
    ext = pl.pallas_call(
        blend_kernel,
        out_shape=jax.ShapeDtypeStruct(full, F32),
        in_specs=[hbm] * 8,
        out_specs=hbm,
        scratch_shapes=[
            pltpu.VMEM(full, F32),
            pltpu.VMEM(beside, F32),
            pltpu.VMEM(beside, F32),
            pltpu.VMEM(full, F32),
            pltpu.VMEM(full, F32),
            pltpu.VMEM((sides, width, listed), BF16),
            pltpu.VMEM(own_cells, I32),
            pltpu.VMEM((2 * HX, 128), I32),
            pltpu.VMEM((2 * HX, 128), I32),
            pltpu.VMEM((8, 2 * HX, 128), I32),
            pltpu.VMEM((2,) + own_cells, I32),
            pltpu.VMEM(tables, I32),
            pltpu.VMEM((sides, rows, 128), F32),
            pltpu.VMEM(message, F32),
            pltpu.VMEM(message, F32),
            pltpu.VMEM(message, F32),
            pltpu.VMEM(message, F32),
            pltpu.VMEM((8,) + message, F32),
            pltpu.VMEM(tables, F32),
            pltpu.VMEM((sides, listed), I32),
            pltpu.SMEM((1, sides), I32),
            pltpu.VMEM((width, hidden), BF16),
            pltpu.VMEM((levels, hidden, hidden), BF16),
            pltpu.VMEM((1, hidden), BF16),
            pltpu.VMEM((levels + 1, 1, hidden), F32),
            pltpu.VMEM((hidden, width), BF16),
            pltpu.VMEM((levels, hidden, hidden), BF16),
            pltpu.VMEM((levels + 1, hidden, 128), F32),
            pltpu.VMEM((2, len(ROUTES), width // ROW_PARTS, listed * ROW_PARTS // len(ROUTES)), BF16),
            dma((7,)), dma((len(ROUTES),)), dma((len(ROUTES),)), dma((2, len(ROUTES))), dma((2, len(ROUTES))),
            dma((sides,)), dma((sides,)),
            dma((8,)), dma((8,)), dma((8,)), dma((8,)), dma((8,)), dma((8,)), dma((full[0] // 8,)),
        ],
        compiler_params=pltpu.CompilerParams(
            collective_id=0, has_side_effects=True, vmem_limit_bytes=61 << 20
        ),
        name="blend",
    )(
        density, feat, band_cell[0, 0], band_count[0], w_in[0, 0], w_hid[0, 0],
        w_out[0], biases[0, 0][:, None, :],
    )
    return pl.pallas_call(
        finish_kernel,
        out_shape=(
            jax.ShapeDtypeStruct(density.shape, F32),
            jax.ShapeDtypeStruct((3,) + density.shape, F32),
        ),
        in_specs=[hbm],
        out_specs=(hbm, hbm),
        scratch_shapes=[
            pltpu.VMEM(full, F32),
            pltpu.VMEM(full, F32),
            pltpu.VMEM(full, F32),
            pltpu.VMEM(density.shape, F32),
            pltpu.VMEM((3,) + density.shape, F32),
            dma((full[0] // 8,)), dma((size_x // 8,)), dma((size_x // 8,)),
        ],
        compiler_params=pltpu.CompilerParams(vmem_limit_bytes=61 << 20),
        name="finish",
    )(ext)


def solution(mesh):
    placed = (
        P("bx", "by", None),
        P("bx", "by", None, None, None),
        P("bx", "by", None, None),
        P("bx", "by", None),
        P("bx", "by", None, None),
        P("bx", "by", None, None, None),
        P("bx", "by", None),
        P("bx", "by", None, None),
    )
    return jax.shard_map(
        shards,
        mesh=mesh,
        in_specs=placed,
        out_specs=(P("bx", "by", None), P(None, "bx", "by", None)),
        check_vma=False,
    )
```

```python
import functools

import jax
import jax.numpy as jnp
from jax import lax
from jax.experimental import pallas as pl
from jax.experimental.pallas import tpu as pltpu
from jax.sharding import PartitionSpec as P

MESH = pl.DeviceIdType.MESH
F32, BF16, I32 = jnp.float32, jnp.bfloat16, jnp.int32
HX, HY = 4, 8
GROUP = 4
ROUTES = (2, 1, 3, 2, 0, 1, 3, 2)
ROW_PARTS = 2
AROUND = ((-1, 0), (1, 0), (0, -1), (0, 1), (-1, -1), (-1, 1), (1, -1), (1, 1))


def spread(row, index):
    wide = jnp.broadcast_to(row, index.shape)
    return jnp.take_along_axis(wide, index, axis=1, mode="promise_in_bounds")


def blend_kernel(
    dens, feat, cell, count, w_in, w_hid, w_out, bias, out,
    field, side_after, side_before, coef_x, coef_y, recv, cells, tile_lo, tile_hi, tiles_in, cells_in, table,
    nets, up, down, left, right, values_in, values,
    cell_v, count_s, win_v, whid_v, wout_v, bias_v, win_t, whid_t, bias_w,
    relayed, load_sem, far_send, far_recv, relay_send, relay_recv, feat_send, feat_recv, dens_send, dens_recv, cell_send, cell_recv, value_send, value_recv, out_sem,
):
    ix, iy = lax.axis_index("bx"), lax.axis_index("by")
    nx, ny = lax.axis_size("bx"), lax.axis_size("by")
    size_x, size_y, size_z = dens.shape
    listed = cell.shape[1]
    rows = listed // 128
    wide = size_x + 2 * HX
    base_2, base_3 = wide, wide + wide // 2

    def there(dx, dy):
        ok_x = jnp.bool_(True) if dx == 0 else (ix + dx >= 0 if dx < 0 else ix + dx < nx)
        ok_y = jnp.bool_(True) if dy == 0 else (iy + dy >= 0 if dy < 0 else iy + dy < ny)
        return ok_x & ok_y

    def at(dx, dy):
        return {"bx": ix + dx, "by": iy + dy}

    loads = [
        pltpu.make_async_copy(src, dst, load_sem.at[n])
        for n, (src, dst) in enumerate(
            ((cell, cell_v), (count, count_s), (w_hid, whid_v), (w_in, win_v), (w_out, wout_v), (bias, bias_v),
             (dens, field.at[pl.ds(HX, size_x), pl.ds(0, size_y), :]))
        )
    ]
    field[0:HX] = jnp.zeros_like(field[0:HX])
    field[HX + size_x :] = jnp.zeros_like(field[HX + size_x :])
    side_after[...] = jnp.zeros_like(side_after)
    side_before[...] = jnp.zeros_like(side_before)
    values_in[...] = jnp.zeros_like(values_in)
    nets[...] = jnp.zeros_like(nets)
    tiles_in[...] = jnp.full_like(tiles_in, -1)
    cells_in[...] = jnp.full_like(cells_in, -1)
    for load in loads:
        load.start()
    place_in = ix % GROUP
    flows = []
    for step, first in ((1, GROUP - 1), (-1, 0)):
        def starts(shift, step=step, first=first):
            origin = ix + shift
            return (origin % GROUP == first) & (origin >= 0) & (origin < nx) & (origin + step >= 0) & (origin + step < nx)

        flows.append((step, 1 if step > 0 else 0, starts))
    behind = sorted({r for r in ROUTES if r})
    expected = sum(there(dx, dy).astype(I32) for dx, dy in AROUND)
    barrier = pltpu.get_barrier_semaphore()
    for dx, dy in AROUND:
        @pl.when(there(dx, dy))
        def _(dx=dx, dy=dy):
            pl.semaphore_signal(barrier, inc=1, device_id=at(dx, dy), device_id_type=MESH)

    for step, _side, starts in flows:
        for r in behind:
            if r > 1:
                @pl.when(starts(r * step))
                def _(r=r, step=step):
                    pl.semaphore_signal(barrier, inc=1, device_id=at(r * step, 0), device_id_type=MESH)

                expected = expected + starts(0).astype(I32)

            @pl.when(starts(-step))
            def _(r=r, step=step):
                pl.semaphore_signal(barrier, inc=1, device_id=at(-(r + 1) * step, 0), device_id_type=MESH)

            expected = expected + starts(r * step).astype(I32)

    loads[0].wait()
    loads[1].wait()
    ranks = lax.broadcasted_iota(I32, (1, listed), 1)
    for s in range(4):
        usable = (ranks < count_s[0, s]) & there(*AROUND[s])
        height = jnp.where(usable, cell_v[s : s + 1, :] & (size_z - 1), -1)
        for r in range(rows):
            cells[s * rows + r : s * rows + r + 1, :] = height[:, r * 128 : (r + 1) * 128]
    pairs = HX // 2
    tile_lo[0:HX] = cells[0:HX]
    tile_hi[0:HX] = cells[2 * rows - HX : 2 * rows]
    for n, s in enumerate((2, 3)):
        tile_lo[HX + n * pairs : HX + (n + 1) * pairs] = cells[s * rows : s * rows + pairs]
        tile_hi[HX + n * pairs : HX + (n + 1) * pairs] = cells[(s + 1) * rows - pairs : (s + 1) * rows]

    def fill(which, source):
        table[which, HX : HX + size_x] = source[0 : 2 * rows]
        for n, base in enumerate((base_2, base_3)):
            table[which, base + pairs : base + pairs + rows] = source[(2 + n) * rows : (3 + n) * rows]

    def fill_strips(which, lo, hi):
        table[which, 0:HX] = lo[0:HX]
        table[which, HX + size_x : wide] = hi[0:HX]
        for n, base in enumerate((base_2, base_3)):
            table[which, base : base + pairs] = lo[HX + n * pairs : HX + (n + 1) * pairs]
            table[which, base + pairs + rows : base + rows + 2 * pairs] = hi[HX + n * pairs : HX + (n + 1) * pairs]

    lane = lax.broadcasted_iota(I32, (8, 128), 1)
    sub = lax.broadcasted_iota(I32, (8, 128), 0)
    groups = size_y // 8
    half = groups // 2
    index = [4 * (8 * g + sub) + lane // 32 for g in range(groups)]
    dist_y = [((8 * g + sub).astype(F32) + 0.5) / size_y - 0.5 for g in range(groups)]
    after = sub < HX

    def both(first, second):
        return jnp.where(after, first, second)

    top = groups - 1
    index_side = both(index[0], index[top])
    index_side_y = [both(index[half * parity], index[top % half + half * parity]) for parity in range(2)]
    dist_side, off_side = both(dist_y[0], dist_y[top]), both(-1.0, 1.0)

    def entries(lists, g, pair, parity):
        def row(which, at_row):
            return lists[which, pl.ds(at_row, 1), :]

        x = 2 * pair + parity
        if g < groups:
            row_y = row(0, (base_2 if g < half else base_3) + pair)
            return spread(row(0, x), index[g]), spread(row_y, index[g % half + half * parity])
        row_x = both(row(2, x), row(1, x))
        row_y = both(row(2, base_2 + pair), row(1, base_3 + pair))
        return spread(row_x, index_side), spread(row_y, index_side_y[parity])

    def prepare(chosen):
        def step(pair, _):
            for parity in range(2):
                x = 2 * pair + parity
                local = (x + size_x - HX) % size_x
                dist_x = (local.astype(F32) + 0.5) / size_x - 0.5
                off_x = jnp.where(local < size_x // 2, -1.0, 1.0)
                for g in chosen:
                    in_x, in_y = entries(table, g, pair, parity)
                    voxels = pl.ds(8 * g, 8)
                    if g < groups:
                        across, off_y = dist_y[g], -1.0 if g < half else 1.0
                        density = field[x, voxels, :]
                    else:
                        across, off_y = dist_side, off_side
                        density = both(side_after[x], side_before[x])
                    sq_x, sq_y = dist_x * dist_x, across * across
                    far_x, far_y = dist_x - off_x, across - off_y
                    own = 1.0 / (sq_x + sq_y + 0.25)
                    w_x = jnp.where(in_x == lane, 1.0 / (far_x * far_x + sq_y + 0.25), 0.0)
                    w_y = jnp.where(in_y == lane, 1.0 / (sq_x + far_y * far_y + 0.25), 0.0)
                    share = 1.0 / (own + w_x + w_y)
                    field[x, voxels, :] = own * density * share
                    coef_x[x, voxels, :] = w_x * share
                    coef_y[x, voxels, :] = w_y * share
            return 0

        return step

    own_groups = tuple(range(groups))
    fill(0, cells)
    for load in loads[2:]:
        load.wait()
    lax.fori_loop(pairs, wide // 2 - pairs, prepare(own_groups), 0)
    for layer in range(w_hid.shape[0]):
        whid_t[layer] = whid_v[layer].T
    win_t[...] = win_v[...].T
    for layer in range(bias.shape[0]):
        bias_w[layer] = jnp.broadcast_to(bias_v[layer], (128, bias.shape[2])).T

    pl.semaphore_wait(barrier, expected)

    def remote(src, dst, send, arrive, n, dx, dy):
        return pltpu.make_async_remote_copy(
            src_ref=src, dst_ref=dst, send_sem=send.at[n], recv_sem=arrive.at[n],
            device_id=at(dx, dy), device_id_type=MESH)

    def opposite(s):
        dx = jnp.where(s == 0, 1, jnp.where(s == 1, -1, 0))
        dy = jnp.where(s == 2, 1, jnp.where(s == 3, -1, 0))
        ok = (ix + dx >= 0) & (ix + dx < nx) & (iy + dy >= 0) & (iy + dy < ny)
        return ok, dx, dy

    def feature_copy(s, dx, dy):
        return remote(feat.at[s], recv.at[s], feat_send, feat_recv, s, dx, dy)

    def density_copy(n, dx, dy):
        if dx == 0:
            src_x, dst_x = pl.ds(0, size_x), pl.ds(HX, size_x)
        elif dx > 0:
            src_x, dst_x = pl.ds(size_x - HX, HX), pl.ds(0, HX)
        else:
            src_x, dst_x = pl.ds(0, HX), pl.ds(HX + size_x, HX)
        if dy == 0:
            src, dst = dens.at[src_x], field.at[dst_x, pl.ds(0, size_y), :]
        elif dy > 0:
            src, dst = dens.at[src_x, pl.ds(size_y - HY, HY), :], side_before.at[dst_x]
        else:
            src, dst = dens.at[src_x, pl.ds(0, HY), :], side_after.at[dst_x]
        return remote(src, dst, dens_send, dens_recv, n, dx, dy)

    def cell_copy(n, dx, dy):
        m = AROUND.index((-dx, -dy))
        if dx == 0:
            return remote(cells, cells_in.at[m - 2], cell_send, cell_recv, n, dx, dy)
        return remote(tile_lo if dx < 0 else tile_hi, tiles_in.at[m], cell_send, cell_recv, n, dx, dy)

    def value_copy(n, dx, dy):
        m = AROUND.index((-dx, -dy))
        src = (left if dy < 0 else right) if dx == 0 else (down if dx < 0 else up)
        return remote(src, values_in.at[m], value_send, value_recv, n, dx, dy)

    part_rows = feat.shape[1] // ROW_PARTS
    part_columns = listed * ROW_PARTS // len(ROUTES)

    def piece(ref, s, n):
        return ref.at[
            s, pl.ds(n % ROW_PARTS * part_rows, part_rows), pl.ds(n // ROW_PARTS * part_columns, part_columns)
        ]

    def far_copy(n, side, step):
        r = ROUTES[n]
        if r:
            dst, arrive, shift = relayed.at[side, n], relay_recv.at[side, n], -r * step
        else:
            dst, arrive, shift = piece(recv, side, n), far_recv.at[n], step
        return pltpu.make_async_remote_copy(
            src_ref=piece(feat, side, n), dst_ref=dst, send_sem=far_send.at[n], recv_sem=arrive,
            device_id=at(shift, 0), device_id_type=MESH)

    def forward_copy(n, side, step):
        return pltpu.make_async_remote_copy(
            src_ref=relayed.at[side, n], dst_ref=piece(recv, side, n), send_sem=relay_send.at[side, n],
            recv_sem=far_recv.at[n], device_id=at((ROUTES[n] + 1) * step, 0), device_id_type=MESH)

    for step, side, starts in flows:
        @pl.when(starts(0))
        def _(step=step, side=side):
            for n in range(len(ROUTES)):
                far_copy(n, side, step).start()

    def near(s):
        ok = there(*AROUND[s])
        for step, side, starts in flows:
            if s == side:
                ok = ok & jnp.logical_not(starts(0))
        return ok

    for s in (2, 3, 0, 1):
        @pl.when(near(s))
        def _(s=s):
            feature_copy(s, *AROUND[s]).start()

    lower = ix < nx // 2
    for (step, side, starts), turn in ((flows[1], lower), (flows[0], True), (flows[1], jnp.logical_not(lower))):
        for n in range(len(ROUTES)):
            if ROUTES[n]:
                @pl.when(starts(ROUTES[n] * step) & turn)
                def _(n=n, step=step, side=side):
                    far_copy(n, side, step).wait_recv()
                    forward_copy(n, side, step).start()

    for n, (dx, dy) in enumerate(AROUND):
        @pl.when(there(dx, dy))
        def _(n=n, dx=dx, dy=dy):
            cell_copy(n, dx, dy).start()
            density_copy(n, dx, dy).start()

    head = jnp.broadcast_to(wout_v[...].astype(F32), (16, w_out.shape[1])).astype(BF16)
    last = ix % 4 == 3

    def evaluate(step, _):
        s = jnp.where(step < 2, step + 2, jnp.where(last, 3 - step, step - 2))
        ok, dx, dy = opposite(s)

        @pl.when(ok)
        def _():
            far = ((s == 1) & flows[0][2](-1)) | ((s == 0) & flows[1][2](1))

            @pl.when(far)
            def _():
                for n in range(len(ROUTES)):
                    pltpu.make_async_remote_copy(
                        src_ref=piece(recv, s, n), dst_ref=piece(recv, s, n), send_sem=far_send.at[n],
                        recv_sem=far_recv.at[n], device_id=at(dx, dy), device_id_type=MESH).wait_recv()

            @pl.when(jnp.logical_not(far))
            def _():
                feature_copy(s, dx, dy).wait_recv()

            def layer(weights, hidden, level):
                column = jnp.concatenate([bias_w[level]] * (listed // 128), axis=1)
                total = jnp.dot(weights, hidden, preferred_element_type=F32) + column
                return jnp.maximum(total.astype(BF16), 0)

            hidden = layer(win_t[...], recv[s], 0)
            for level in range(whid_t.shape[0]):
                hidden = layer(whid_t[level], hidden, level + 1)
            raw = jnp.dot(head, hidden, preferred_element_type=F32)[0:1, :]
            result = jnp.maximum(raw, 0.0) + jnp.log1p(jnp.exp(-jnp.abs(raw)))
            for r in range(rows):
                nets[s, r : r + 1, :] = result[:, r * 128 : (r + 1) * 128]

        return 0

    lax.fori_loop(0, 4, evaluate, 0)

    up[0:rows] = nets[0]
    down[0:rows] = nets[1]
    left[0:rows] = nets[3]
    right[0:rows] = nets[2]
    for n, s in enumerate((2, 3)):
        up[rows + n * pairs : rows + (n + 1) * pairs] = nets[s, rows - pairs : rows]
        down[rows + n * pairs : rows + (n + 1) * pairs] = nets[s, 0:pairs]
    for side in (left, right):
        side[rows : rows + HX] = nets[0, 0:HX]
        side[rows + HX : rows + 2 * HX] = nets[1, rows - HX : rows]
    for n, (dx, dy) in enumerate(AROUND):
        @pl.when(there(dx, dy))
        def _(n=n, dx=dx, dy=dy):
            value_copy(n, dx, dy).start()

    for n, (dx, dy) in enumerate(AROUND):
        @pl.when(there(-dx, -dy))
        def _(n=n, dx=dx, dy=dy):
            cell_copy(n, dx, dy).wait_recv()
            density_copy(n, dx, dy).wait_recv()

    fill(1, cells_in.at[0])
    fill(2, cells_in.at[1])
    fill_strips(0, tiles_in.at[0], tiles_in.at[1])
    fill_strips(1, tiles_in.at[4], tiles_in.at[6])
    fill_strips(2, tiles_in.at[5], tiles_in.at[7])
    lax.fori_loop(0, pairs, prepare(own_groups), 0, unroll=True)
    lax.fori_loop(wide // 2 - pairs, wide // 2, prepare(own_groups), 0, unroll=True)
    lax.fori_loop(0, wide // 2, prepare((groups,)), 0, unroll=5)

    def arrived(along):
        for n, (dx, dy) in enumerate(AROUND):
            if -dx == along:
                @pl.when(there(-dx, -dy))
                def _(n=n, dx=dx, dy=dy):
                    value_copy(n, dx, dy).wait_recv()

    def put(which, first, source):
        values[which, first : first + source.shape[0]] = source

    tail, strip = HX + size_x, rows
    lo_2, hi_2 = base_2 + pairs, base_2 + pairs + rows
    lo_3, hi_3 = base_3 + pairs, base_3 + pairs + rows
    west, east, south, north = (values_in.at[m] for m in range(4))
    south_west, north_west, south_east, north_east = (values_in.at[m] for m in range(4, 8))
    put(0, 0, nets[1, rows - HX : rows])
    put(0, tail, nets[0, 0:HX])
    put(1, lo_3, nets[3])
    put(2, lo_2, nets[2])
    arrived(0)
    put(0, lo_2, south[0:rows])
    put(0, lo_3, north[0:rows])
    for which, column in ((1, south), (2, north)):
        put(which, 0, column[strip + HX : strip + 2 * HX])
        put(which, tail, column[strip : strip + HX])

    def result_copy(chunk):
        part = pl.ds(4 * chunk, 4)
        return pltpu.make_async_copy(field.at[part], out.at[part], out_sem.at[chunk])

    def blend(chunk):
        for k in range(4):
            pair, parity = 2 * chunk + k // 2, k % 2
            x = 4 * chunk + k
            for g in range(groups + 1):
                from_x, from_y = entries(values, g, pair, parity)
                voxels = pl.ds(8 * g, 8)
                field[x, voxels, :] = (
                    field[x, voxels, :] + coef_x[x, voxels, :] * from_x + coef_y[x, voxels, :] * from_y
                )
        result_copy(chunk).start()

    chunks = wide // 4

    def blend_half(turn, _):
        upper = jnp.where(place_in == 0, 1 - turn, turn)

        @pl.when(upper == 0)
        def _():
            arrived(-1)
            put(0, HX, west[0:rows])
            put(0, base_2, south_west[strip : strip + pairs])
            put(0, base_3, north_west[strip + pairs : strip + 2 * pairs])
            put(1, HX, south_west[0:rows])
            put(2, HX, north_west[0:rows])
            put(1, base_3, west[strip + pairs : strip + 2 * pairs])
            put(2, base_2, west[strip : strip + pairs])

        @pl.when(upper == 1)
        def _():
            arrived(1)
            put(0, HX + rows, east[0:rows])
            put(0, hi_2, south_east[strip : strip + pairs])
            put(0, hi_3, north_east[strip + pairs : strip + 2 * pairs])
            put(1, HX + rows, south_east[0:rows])
            put(2, HX + rows, north_east[0:rows])
            put(1, hi_3, east[strip + pairs : strip + 2 * pairs])
            put(2, hi_2, east[strip : strip + pairs])

        def step(k, _):
            blend(chunks // 2 * upper + k)
            return 0

        lax.fori_loop(0, chunks // 2, step, 0, unroll=True)
        return 0

    lax.fori_loop(0, 2, blend_half, 0)

    for s in range(4):
        @pl.when(near(s))
        def _(s=s):
            feature_copy(s, *AROUND[s]).wait_send()

    for step, side, starts in flows:
        @pl.when(starts(0))
        def _(step=step, side=side):
            for n in range(len(ROUTES)):
                far_copy(n, side, step).wait_send()

        for n in range(len(ROUTES)):
            if ROUTES[n]:
                @pl.when(starts(ROUTES[n] * step))
                def _(n=n, step=step, side=side):
                    forward_copy(n, side, step).wait_send()

    for n, (dx, dy) in enumerate(AROUND):
        @pl.when(there(dx, dy))
        def _(n=n, dx=dx, dy=dy):
            cell_copy(n, dx, dy).wait_send()
            density_copy(n, dx, dy).wait_send()
            value_copy(n, dx, dy).wait_send()
    for chunk in range(chunks):
        result_copy(chunk).wait()


def finish_kernel(ext, smoothed, normals, zero, one, two, soft, grads, load_sem, soft_sem, grad_sem):
    ix, iy = lax.axis_index("bx"), lax.axis_index("by")
    nx, ny = lax.axis_size("bx"), lax.axis_size("by")
    size_x, size_y, size_z = smoothed.shape
    full_x, full_y = size_x + 2 * HX, size_y + HY
    chunks = full_x // 8

    def load(chunk):
        part = pl.ds(8 * chunk, 8)
        return pltpu.make_async_copy(ext.at[part], zero.at[part], load_sem.at[chunk])

    def store(chunk):
        part = pl.ds(8 * chunk, 8)
        return (
            pltpu.make_async_copy(soft.at[part], smoothed.at[part], soft_sem.at[chunk]),
            pltpu.make_async_copy(grads.at[:, part], normals.at[:, part], grad_sem.at[chunk]),
        )

    for chunk in range(chunks):
        load(chunk).start()
    sub = lax.broadcasted_iota(I32, (full_y, size_z), 0)
    inside_y = (sub < size_y) | ((sub < size_y + HX) & (iy < ny - 1)) | ((sub >= size_y + HX) & (iy > 0))
    keep_y = jnp.where(inside_y, 0.2, 0.0)

    def one_pass(src, dst, first, end):
        def step(x, _):
            centre = src[x]
            total = (
                centre + src[x + 1] + src[x - 1]
                + pltpu.roll(centre, 1, 0) + pltpu.roll(centre, full_y - 1, 0)
            )
            inside = ((x >= HX) | (ix > 0)) & ((x < HX + size_x) | (ix < nx - 1))
            dst[x] = total * jnp.where(inside, keep_y, 0.0)
            return 0

        lax.fori_loop(first, end, step, 0, unroll=4)

    for chunk in range(chunks):
        load(chunk).wait()
        one_pass(zero, one, max(1, 8 * chunk - 1), 8 * chunk + 7)
    one_pass(one, two, 2, full_x - 2)
    one_pass(two, one, 3, full_x - 3)
    last_z = lax.broadcasted_iota(I32, (size_y, size_z), 1)

    def gradient(chunk, _):
        for k in range(8):
            x = 8 * chunk + k
            row = HX + x
            centre = one[row]
            own = centre[0:size_y]
            grad_x = one[row + 1, 0:size_y, :] - one[row - 1, 0:size_y, :]
            grad_y = (pltpu.roll(centre, full_y - 1, 0) - pltpu.roll(centre, 1, 0))[0:size_y]
            ahead = jnp.where(last_z == size_z - 1, 0.0, pltpu.roll(own, size_z - 1, 1))
            behind = jnp.where(last_z == 0, 0.0, pltpu.roll(own, 1, 1))
            grad_z = ahead - behind
            factor = lax.rsqrt(1.0 + grad_x * grad_x + grad_y * grad_y + grad_z * grad_z)
            soft[x] = own
            grads[0, x] = grad_x * factor
            grads[1, x] = grad_y * factor
            grads[2, x] = grad_z * factor
        for copy in store(chunk):
            copy.start()
        return 0

    lax.fori_loop(0, size_x // 8, gradient, 0)
    for chunk in range(size_x // 8):
        for copy in store(chunk):
            copy.wait()


def shards(density, band_feat, band_cell, band_count, w_in, w_hid, w_out, biases):
    size_x, size_y, size_z = density.shape
    feat = jnp.swapaxes(band_feat[0, 0], 1, 2)
    sides, width, listed = feat.shape
    levels, hidden = w_hid.shape[2], w_hid.shape[3]
    rows = listed // 128
    full = (size_x + 2 * HX, size_y + HY, size_z)
    beside = (size_x + 2 * HX, HY, size_z)
    hbm = pl.BlockSpec(memory_space=pltpu.HBM)
    dma = pltpu.SemaphoreType.DMA
    own_cells = (sides * rows, 128)
    message = (rows + 2 * HX, 128)
    tables = (3, 2 * full[0], 128)
    ext = pl.pallas_call(
        blend_kernel,
        out_shape=jax.ShapeDtypeStruct(full, F32),
        in_specs=[hbm] * 8,
        out_specs=hbm,
        scratch_shapes=[
            pltpu.VMEM(full, F32),
            pltpu.VMEM(beside, F32),
            pltpu.VMEM(beside, F32),
            pltpu.VMEM(full, F32),
            pltpu.VMEM(full, F32),
            pltpu.VMEM((sides, width, listed), BF16),
            pltpu.VMEM(own_cells, I32),
            pltpu.VMEM((2 * HX, 128), I32),
            pltpu.VMEM((2 * HX, 128), I32),
            pltpu.VMEM((8, 2 * HX, 128), I32),
            pltpu.VMEM((2,) + own_cells, I32),
            pltpu.VMEM(tables, I32),
            pltpu.VMEM((sides, rows, 128), F32),
            pltpu.VMEM(message, F32),
            pltpu.VMEM(message, F32),
            pltpu.VMEM(message, F32),
            pltpu.VMEM(message, F32),
            pltpu.VMEM((8,) + message, F32),
            pltpu.VMEM(tables, F32),
            pltpu.VMEM((sides, listed), I32),
            pltpu.SMEM((1, sides), I32),
            pltpu.VMEM((width, hidden), BF16),
            pltpu.VMEM((levels, hidden, hidden), BF16),
            pltpu.VMEM((1, hidden), BF16),
            pltpu.VMEM((levels + 1, 1, hidden), F32),
            pltpu.VMEM((hidden, width), BF16),
            pltpu.VMEM((levels, hidden, hidden), BF16),
            pltpu.VMEM((levels + 1, hidden, 128), F32),
            pltpu.VMEM((2, len(ROUTES), width // ROW_PARTS, listed * ROW_PARTS // len(ROUTES)), BF16),
            dma((7,)), dma((len(ROUTES),)), dma((len(ROUTES),)), dma((2, len(ROUTES))), dma((2, len(ROUTES))),
            dma((sides,)), dma((sides,)),
            dma((8,)), dma((8,)), dma((8,)), dma((8,)), dma((8,)), dma((8,)), dma((full[0] // 4,)),
        ],
        compiler_params=pltpu.CompilerParams(
            collective_id=0, has_side_effects=True, vmem_limit_bytes=61 << 20
        ),
        name="blend",
    )(
        density, feat, band_cell[0, 0], band_count[0], w_in[0, 0], w_hid[0, 0],
        w_out[0], biases[0, 0][:, None, :],
    )
    return pl.pallas_call(
        finish_kernel,
        out_shape=(
            jax.ShapeDtypeStruct(density.shape, F32),
            jax.ShapeDtypeStruct((3,) + density.shape, F32),
        ),
        in_specs=[hbm],
        out_specs=(hbm, hbm),
        scratch_shapes=[
            pltpu.VMEM(full, F32),
            pltpu.VMEM(full, F32),
            pltpu.VMEM(full, F32),
            pltpu.VMEM(density.shape, F32),
            pltpu.VMEM((3,) + density.shape, F32),
            dma((full[0] // 8,)), dma((size_x // 8,)), dma((size_x // 8,)),
        ],
        compiler_params=pltpu.CompilerParams(vmem_limit_bytes=61 << 20),
        name="finish",
    )(ext)


def solution(mesh):
    placed = (
        P("bx", "by", None),
        P("bx", "by", None, None, None),
        P("bx", "by", None, None),
        P("bx", "by", None),
        P("bx", "by", None, None),
        P("bx", "by", None, None, None),
        P("bx", "by", None),
        P("bx", "by", None, None),
    )
    return jax.shard_map(
        shards,
        mesh=mesh,
        in_specs=placed,
        out_specs=(P("bx", "by", None), P(None, "bx", "by", None)),
        check_vma=False,
    )
```

```python
import functools

import jax
import jax.numpy as jnp
from jax import lax
from jax.experimental import pallas as pl
from jax.experimental.pallas import tpu as pltpu
from jax.sharding import PartitionSpec as P

MESH = pl.DeviceIdType.MESH
F32, BF16, I32 = jnp.float32, jnp.bfloat16, jnp.int32
HX, HY = 4, 8
GROUP = 4
ROUTES = (2, 1, 3, 2, 0, 1, 3, 2)
ROW_PARTS = 2
AROUND = ((-1, 0), (1, 0), (0, -1), (0, 1), (-1, -1), (-1, 1), (1, -1), (1, 1))


def spread(row, index):
    wide = jnp.broadcast_to(row, index.shape)
    return jnp.take_along_axis(wide, index, axis=1, mode="promise_in_bounds")


def blend_kernel(
    dens, feat, cell, count, w_in, w_hid, w_out, bias, out,
    field, side_after, side_before, coef_x, coef_y, recv, cells, tile_lo, tile_hi, tiles_in, cells_in, table,
    nets, up, down, left, right, corner_out, corner_in, values_in, values,
    cell_v, count_s, win_v, whid_v, wout_v, bias_v, win_t, whid_t, bias_w,
    relayed, load_sem, far_send, far_recv, relay_send, relay_recv, feat_send, feat_recv, dens_send, dens_recv, cell_send, cell_recv, value_send, value_recv, out_sem,
):
    ix, iy = lax.axis_index("bx"), lax.axis_index("by")
    nx, ny = lax.axis_size("bx"), lax.axis_size("by")
    size_x, size_y, size_z = dens.shape
    listed = cell.shape[1]
    rows = listed // 128
    wide = size_x + 2 * HX
    base_2, base_3 = wide, wide + wide // 2

    def there(dx, dy):
        ok_x = jnp.bool_(True) if dx == 0 else (ix + dx >= 0 if dx < 0 else ix + dx < nx)
        ok_y = jnp.bool_(True) if dy == 0 else (iy + dy >= 0 if dy < 0 else iy + dy < ny)
        return ok_x & ok_y

    def at(dx, dy):
        return {"bx": ix + dx, "by": iy + dy}

    loads = [
        pltpu.make_async_copy(src, dst, load_sem.at[n])
        for n, (src, dst) in enumerate(
            ((cell, cell_v), (count, count_s), (w_hid, whid_v), (w_in, win_v), (w_out, wout_v), (bias, bias_v),
             (dens, field.at[pl.ds(HX, size_x), pl.ds(0, size_y), :]))
        )
    ]
    field[0:HX] = jnp.zeros_like(field[0:HX])
    field[HX + size_x :] = jnp.zeros_like(field[HX + size_x :])
    side_after[...] = jnp.zeros_like(side_after)
    side_before[...] = jnp.zeros_like(side_before)
    values_in[...] = jnp.zeros_like(values_in)
    corner_in[...] = jnp.zeros_like(corner_in)
    nets[...] = jnp.zeros_like(nets)
    tiles_in[...] = jnp.full_like(tiles_in, -1)
    cells_in[...] = jnp.full_like(cells_in, -1)
    for load in loads:
        load.start()
    place_in = ix % GROUP
    flows = []
    for step, first in ((1, GROUP - 1), (-1, 0)):
        def starts(shift, step=step, first=first):
            origin = ix + shift
            return (origin % GROUP == first) & (origin >= 0) & (origin < nx) & (origin + step >= 0) & (origin + step < nx)

        flows.append((step, 1 if step > 0 else 0, starts))
    behind = sorted({r for r in ROUTES if r})
    expected = sum(there(dx, dy).astype(I32) for dx, dy in AROUND)
    barrier = pltpu.get_barrier_semaphore()
    for dx, dy in AROUND:
        @pl.when(there(dx, dy))
        def _(dx=dx, dy=dy):
            pl.semaphore_signal(barrier, inc=1, device_id=at(dx, dy), device_id_type=MESH)

    for step, _side, starts in flows:
        for r in behind:
            if r > 1:
                @pl.when(starts(r * step))
                def _(r=r, step=step):
                    pl.semaphore_signal(barrier, inc=1, device_id=at(r * step, 0), device_id_type=MESH)

                expected = expected + starts(0).astype(I32)

            @pl.when(starts(-step))
            def _(r=r, step=step):
                pl.semaphore_signal(barrier, inc=1, device_id=at(-(r + 1) * step, 0), device_id_type=MESH)

            expected = expected + starts(r * step).astype(I32)

    loads[0].wait()
    loads[1].wait()
    ranks = lax.broadcasted_iota(I32, (1, listed), 1)
    for s in range(4):
        usable = (ranks < count_s[0, s]) & there(*AROUND[s])
        height = jnp.where(usable, cell_v[s : s + 1, :] & (size_z - 1), -1)
        for r in range(rows):
            cells[s * rows + r : s * rows + r + 1, :] = height[:, r * 128 : (r + 1) * 128]
    pairs = HX // 2
    tile_lo[0:HX] = cells[0:HX]
    tile_hi[0:HX] = cells[2 * rows - HX : 2 * rows]
    for n, s in enumerate((2, 3)):
        tile_lo[HX + n * pairs : HX + (n + 1) * pairs] = cells[s * rows : s * rows + pairs]
        tile_hi[HX + n * pairs : HX + (n + 1) * pairs] = cells[(s + 1) * rows - pairs : (s + 1) * rows]

    def fill(which, source):
        table[which, HX : HX + size_x] = source[0 : 2 * rows]
        for n, base in enumerate((base_2, base_3)):
            table[which, base + pairs : base + pairs + rows] = source[(2 + n) * rows : (3 + n) * rows]

    def fill_strips(which, lo, hi):
        table[which, 0:HX] = lo[0:HX]
        table[which, HX + size_x : wide] = hi[0:HX]
        for n, base in enumerate((base_2, base_3)):
            table[which, base : base + pairs] = lo[HX + n * pairs : HX + (n + 1) * pairs]
            table[which, base + pairs + rows : base + rows + 2 * pairs] = hi[HX + n * pairs : HX + (n + 1) * pairs]

    lane = lax.broadcasted_iota(I32, (8, 128), 1)
    sub = lax.broadcasted_iota(I32, (8, 128), 0)
    groups = size_y // 8
    half = groups // 2
    index = [4 * (8 * g + sub) + lane // 32 for g in range(groups)]
    dist_y = [((8 * g + sub).astype(F32) + 0.5) / size_y - 0.5 for g in range(groups)]
    after = sub < HX

    def both(first, second):
        return jnp.where(after, first, second)

    top = groups - 1
    index_side = both(index[0], index[top])
    index_side_y = [both(index[half * parity], index[top % half + half * parity]) for parity in range(2)]
    dist_side, off_side = both(dist_y[0], dist_y[top]), both(-1.0, 1.0)

    def entries(lists, g, pair, parity):
        def row(which, at_row):
            return lists[which, pl.ds(at_row, 1), :]

        x = 2 * pair + parity
        if g < groups:
            row_y = row(0, (base_2 if g < half else base_3) + pair)
            return spread(row(0, x), index[g]), spread(row_y, index[g % half + half * parity])
        row_x = both(row(2, x), row(1, x))
        row_y = both(row(2, base_2 + pair), row(1, base_3 + pair))
        return spread(row_x, index_side), spread(row_y, index_side_y[parity])

    def prepare(chosen):
        def step(pair, _):
            for parity in range(2):
                x = 2 * pair + parity
                local = (x + size_x - HX) % size_x
                dist_x = (local.astype(F32) + 0.5) / size_x - 0.5
                off_x = jnp.where(local < size_x // 2, -1.0, 1.0)
                for g in chosen:
                    in_x, in_y = entries(table, g, pair, parity)
                    voxels = pl.ds(8 * g, 8)
                    if g < groups:
                        across, off_y = dist_y[g], -1.0 if g < half else 1.0
                        density = field[x, voxels, :]
                    else:
                        across, off_y = dist_side, off_side
                        density = both(side_after[x], side_before[x])
                    sq_x, sq_y = dist_x * dist_x, across * across
                    far_x, far_y = dist_x - off_x, across - off_y
                    own = 1.0 / (sq_x + sq_y + 0.25)
                    w_x = jnp.where(in_x == lane, 1.0 / (far_x * far_x + sq_y + 0.25), 0.0)
                    w_y = jnp.where(in_y == lane, 1.0 / (sq_x + far_y * far_y + 0.25), 0.0)
                    share = 1.0 / (own + w_x + w_y)
                    field[x, voxels, :] = own * density * share
                    coef_x[x, voxels, :] = w_x * share
                    coef_y[x, voxels, :] = w_y * share
            return 0

        return step

    own_groups = tuple(range(groups))
    fill(0, cells)
    for load in loads[2:]:
        load.wait()
    lax.fori_loop(pairs, wide // 2 - pairs, prepare(own_groups), 0)
    for layer in range(w_hid.shape[0]):
        whid_t[layer] = whid_v[layer].T
    win_t[...] = win_v[...].T
    for layer in range(bias.shape[0]):
        bias_w[layer] = jnp.broadcast_to(bias_v[layer], (128, bias.shape[2])).T

    pl.semaphore_wait(barrier, expected)

    def remote(src, dst, send, arrive, n, dx, dy):
        return pltpu.make_async_remote_copy(
            src_ref=src, dst_ref=dst, send_sem=send.at[n], recv_sem=arrive.at[n],
            device_id=at(dx, dy), device_id_type=MESH)

    def opposite(s):
        dx = jnp.where(s == 0, 1, jnp.where(s == 1, -1, 0))
        dy = jnp.where(s == 2, 1, jnp.where(s == 3, -1, 0))
        ok = (ix + dx >= 0) & (ix + dx < nx) & (iy + dy >= 0) & (iy + dy < ny)
        return ok, dx, dy

    def feature_copy(s, dx, dy):
        return remote(feat.at[s], recv.at[s], feat_send, feat_recv, s, dx, dy)

    def density_copy(n, dx, dy):
        if dx == 0:
            src_x, dst_x = pl.ds(0, size_x), pl.ds(HX, size_x)
        elif dx > 0:
            src_x, dst_x = pl.ds(size_x - HX, HX), pl.ds(0, HX)
        else:
            src_x, dst_x = pl.ds(0, HX), pl.ds(HX + size_x, HX)
        if dy == 0:
            src, dst = dens.at[src_x], field.at[dst_x, pl.ds(0, size_y), :]
        elif dy > 0:
            src, dst = dens.at[src_x, pl.ds(size_y - HY, HY), :], side_before.at[dst_x]
        else:
            src, dst = dens.at[src_x, pl.ds(0, HY), :], side_after.at[dst_x]
        return remote(src, dst, dens_send, dens_recv, n, dx, dy)

    def cell_copy(n, dx, dy):
        m = AROUND.index((-dx, -dy))
        if dx == 0:
            return remote(cells, cells_in.at[m - 2], cell_send, cell_recv, n, dx, dy)
        return remote(tile_lo if dx < 0 else tile_hi, tiles_in.at[m], cell_send, cell_recv, n, dx, dy)

    def value_copy(n, dx, dy):
        m = AROUND.index((-dx, -dy))
        if dx and dy:
            return remote(corner_out.at[n - 4], corner_in.at[m - 4], value_send, value_recv, n, dx, dy)
        src = (left if dy < 0 else right) if dx == 0 else (down if dx < 0 else up)
        return remote(src, values_in.at[m], value_send, value_recv, n, dx, dy)

    part_rows = feat.shape[1] // ROW_PARTS
    part_columns = listed * ROW_PARTS // len(ROUTES)

    def piece(ref, s, n):
        return ref.at[
            s, pl.ds(n % ROW_PARTS * part_rows, part_rows), pl.ds(n // ROW_PARTS * part_columns, part_columns)
        ]

    def far_copy(n, side, step):
        r = ROUTES[n]
        if r:
            dst, arrive, shift = relayed.at[side, n], relay_recv.at[side, n], -r * step
        else:
            dst, arrive, shift = piece(recv, side, n), far_recv.at[n], step
        return pltpu.make_async_remote_copy(
            src_ref=piece(feat, side, n), dst_ref=dst, send_sem=far_send.at[n], recv_sem=arrive,
            device_id=at(shift, 0), device_id_type=MESH)

    def forward_copy(n, side, step):
        return pltpu.make_async_remote_copy(
            src_ref=relayed.at[side, n], dst_ref=piece(recv, side, n), send_sem=relay_send.at[side, n],
            recv_sem=far_recv.at[n], device_id=at((ROUTES[n] + 1) * step, 0), device_id_type=MESH)

    for step, side, starts in flows:
        @pl.when(starts(0))
        def _(step=step, side=side):
            for n in range(len(ROUTES)):
                far_copy(n, side, step).start()

    def near(s):
        ok = there(*AROUND[s])
        for step, side, starts in flows:
            if s == side:
                ok = ok & jnp.logical_not(starts(0))
        return ok

    for s in (2, 3, 0, 1):
        @pl.when(near(s))
        def _(s=s):
            feature_copy(s, *AROUND[s]).start()

    lower = ix < nx // 2
    for (step, side, starts), turn in ((flows[1], lower), (flows[0], True), (flows[1], jnp.logical_not(lower))):
        for n in range(len(ROUTES)):
            if ROUTES[n]:
                @pl.when(starts(ROUTES[n] * step) & turn)
                def _(n=n, step=step, side=side):
                    far_copy(n, side, step).wait_recv()
                    forward_copy(n, side, step).start()

    for n, (dx, dy) in enumerate(AROUND):
        @pl.when(there(dx, dy))
        def _(n=n, dx=dx, dy=dy):
            cell_copy(n, dx, dy).start()
            density_copy(n, dx, dy).start()

    head = jnp.broadcast_to(wout_v[...].astype(F32), (16, w_out.shape[1])).astype(BF16)
    last = ix % 4 == 3

    def evaluate(step, _):
        s = jnp.where(step < 2, step + 2, jnp.where(last, 3 - step, step - 2))
        ok, dx, dy = opposite(s)

        @pl.when(ok)
        def _():
            far = ((s == 1) & flows[0][2](-1)) | ((s == 0) & flows[1][2](1))

            @pl.when(far)
            def _():
                for n in range(len(ROUTES)):
                    pltpu.make_async_remote_copy(
                        src_ref=piece(recv, s, n), dst_ref=piece(recv, s, n), send_sem=far_send.at[n],
                        recv_sem=far_recv.at[n], device_id=at(dx, dy), device_id_type=MESH).wait_recv()

            @pl.when(jnp.logical_not(far))
            def _():
                feature_copy(s, dx, dy).wait_recv()

            def layer(weights, hidden, level):
                column = jnp.concatenate([bias_w[level]] * (listed // 128), axis=1)
                total = jnp.dot(weights, hidden, preferred_element_type=F32) + column
                return jnp.maximum(total.astype(BF16), 0)

            hidden = layer(win_t[...], recv[s], 0)
            for level in range(whid_t.shape[0]):
                hidden = layer(whid_t[level], hidden, level + 1)
            raw = jnp.dot(head, hidden, preferred_element_type=F32)[0:1, :]
            result = jnp.maximum(raw, 0.0) + jnp.log1p(jnp.exp(-jnp.abs(raw)))
            for r in range(rows):
                nets[s, r : r + 1, :] = result[:, r * 128 : (r + 1) * 128]

        return 0

    lax.fori_loop(0, 4, evaluate, 0)

    up[0:rows] = nets[0]
    down[0:rows] = nets[1]
    left[0:rows] = nets[3]
    right[0:rows] = nets[2]
    for n, s in enumerate((2, 3)):
        up[rows + n * pairs : rows + (n + 1) * pairs] = nets[s, rows - pairs : rows]
        down[rows + n * pairs : rows + (n + 1) * pairs] = nets[s, 0:pairs]
    for side in (left, right):
        side[rows : rows + HX] = nets[0, 0:HX]
        side[rows + HX : rows + 2 * HX] = nets[1, rows - HX : rows]
    first_half = lax.broadcasted_iota(I32, (1, 128), 1) < 64
    for n in range(4, 8):
        dx, dy = AROUND[n]
        along, beside = (0 if dx > 0 else 1), (2 if dy > 0 else 3)
        edge = 4 * HX
        shift = 128 - edge if dy > 0 else edge
        near_edge = lane >= 128 - edge if dy > 0 else lane < edge
        corner_out[n - 4] = jnp.where(near_edge, nets[along, 0:8], pltpu.roll(nets[along, 8:16], shift, 1))
        for k in range(pairs):
            at_row = rows - pairs + k if dx > 0 else k
            line = nets[beside, at_row : at_row + 1, :]
            turned = pltpu.roll(line, 64, 1)
            kept = first_half if dy > 0 else jnp.logical_not(first_half)
            for h, value in enumerate((line, turned) if dy > 0 else (turned, line)):
                to = 2 * k + h
                corner_out[n - 4, to : to + 1, :] = jnp.where(kept, value, corner_out[n - 4, to : to + 1, :])

    def unpacked(m):
        tile = corner_in[m - 4]
        low = AROUND[m][1] < 0
        lines = []
        for k in range(pairs):
            one, two = tile[2 * k : 2 * k + 1], tile[2 * k + 1 : 2 * k + 2]
            if low:
                lines.append(jnp.where(first_half, one, pltpu.roll(two, 64, 1)))
            else:
                lines.append(jnp.where(first_half, pltpu.roll(one, 64, 1), two))
        return tile, pltpu.roll(tile, 4 * HX if low else 128 - 4 * HX, 1), lines

    for n, (dx, dy) in enumerate(AROUND):
        @pl.when(there(dx, dy))
        def _(n=n, dx=dx, dy=dy):
            value_copy(n, dx, dy).start()

    for n, (dx, dy) in enumerate(AROUND):
        @pl.when(there(-dx, -dy))
        def _(n=n, dx=dx, dy=dy):
            cell_copy(n, dx, dy).wait_recv()
            density_copy(n, dx, dy).wait_recv()

    fill(1, cells_in.at[0])
    fill(2, cells_in.at[1])
    fill_strips(0, tiles_in.at[0], tiles_in.at[1])
    fill_strips(1, tiles_in.at[4], tiles_in.at[6])
    fill_strips(2, tiles_in.at[5], tiles_in.at[7])
    lax.fori_loop(0, pairs, prepare(own_groups), 0, unroll=True)
    lax.fori_loop(wide // 2 - pairs, wide // 2, prepare(own_groups), 0, unroll=True)
    lax.fori_loop(0, wide // 2, prepare((groups,)), 0, unroll=5)

    def arrived(along):
        for n, (dx, dy) in enumerate(AROUND):
            if -dx == along:
                @pl.when(there(-dx, -dy))
                def _(n=n, dx=dx, dy=dy):
                    value_copy(n, dx, dy).wait_recv()

    def put(which, first, source):
        values[which, first : first + source.shape[0]] = source

    tail, strip = HX + size_x, rows
    lo_2, hi_2 = base_2 + pairs, base_2 + pairs + rows
    lo_3, hi_3 = base_3 + pairs, base_3 + pairs + rows
    west, east, south, north = (values_in.at[m] for m in range(4))

    def put_corner(m, which, base, at_x, at_pair):
        head_rows, tail_rows, lines = unpacked(m)
        put(which, at_x, head_rows)
        put(which, at_x + 8, tail_rows)
        for k, line in enumerate(lines):
            put(0, base + at_pair + k, line)

    put(0, 0, nets[1, rows - HX : rows])
    put(0, tail, nets[0, 0:HX])
    put(1, lo_3, nets[3])
    put(2, lo_2, nets[2])
    arrived(0)
    put(0, lo_2, south[0:rows])
    put(0, lo_3, north[0:rows])
    for which, column in ((1, south), (2, north)):
        put(which, 0, column[strip + HX : strip + 2 * HX])
        put(which, tail, column[strip : strip + HX])

    def result_copy(chunk):
        part = pl.ds(4 * chunk, 4)
        return pltpu.make_async_copy(field.at[part], out.at[part], out_sem.at[chunk])

    def blend(chunk):
        for k in range(4):
            pair, parity = 2 * chunk + k // 2, k % 2
            x = 4 * chunk + k
            for g in range(groups + 1):
                from_x, from_y = entries(values, g, pair, parity)
                voxels = pl.ds(8 * g, 8)
                field[x, voxels, :] = (
                    field[x, voxels, :] + coef_x[x, voxels, :] * from_x + coef_y[x, voxels, :] * from_y
                )
        result_copy(chunk).start()

    chunks = wide // 4

    def blend_half(turn, _):
        upper = jnp.where(place_in == 0, 1 - turn, turn)

        @pl.when(upper == 0)
        def _():
            arrived(-1)
            put(0, HX, west[0:rows])
            put_corner(4, 1, base_2, HX, 0)
            put_corner(5, 2, base_3, HX, 0)
            put(1, base_3, west[strip + pairs : strip + 2 * pairs])
            put(2, base_2, west[strip : strip + pairs])

        @pl.when(upper == 1)
        def _():
            arrived(1)
            put(0, HX + rows, east[0:rows])
            put_corner(6, 1, base_2, HX + rows, pairs + rows)
            put_corner(7, 2, base_3, HX + rows, pairs + rows)
            put(1, hi_3, east[strip + pairs : strip + 2 * pairs])
            put(2, hi_2, east[strip : strip + pairs])

        def step(k, _):
            blend(chunks // 2 * upper + k)
            return 0

        lax.fori_loop(0, chunks // 2, step, 0, unroll=True)
        return 0

    lax.fori_loop(0, 2, blend_half, 0)

    for s in range(4):
        @pl.when(near(s))
        def _(s=s):
            feature_copy(s, *AROUND[s]).wait_send()

    for step, side, starts in flows:
        @pl.when(starts(0))
        def _(step=step, side=side):
            for n in range(len(ROUTES)):
                far_copy(n, side, step).wait_send()

        for n in range(len(ROUTES)):
            if ROUTES[n]:
                @pl.when(starts(ROUTES[n] * step))
                def _(n=n, step=step, side=side):
                    forward_copy(n, side, step).wait_send()

    for n, (dx, dy) in enumerate(AROUND):
        @pl.when(there(dx, dy))
        def _(n=n, dx=dx, dy=dy):
            cell_copy(n, dx, dy).wait_send()
            density_copy(n, dx, dy).wait_send()
            value_copy(n, dx, dy).wait_send()
    for chunk in range(chunks):
        result_copy(chunk).wait()


def finish_kernel(ext, smoothed, normals, zero, one, two, soft, grads, load_sem, soft_sem, grad_sem):
    ix, iy = lax.axis_index("bx"), lax.axis_index("by")
    nx, ny = lax.axis_size("bx"), lax.axis_size("by")
    size_x, size_y, size_z = smoothed.shape
    full_x, full_y = size_x + 2 * HX, size_y + HY
    chunks = full_x // 8

    def load(chunk):
        part = pl.ds(8 * chunk, 8)
        return pltpu.make_async_copy(ext.at[part], zero.at[part], load_sem.at[chunk])

    def store(chunk):
        part = pl.ds(8 * chunk, 8)
        return (
            pltpu.make_async_copy(soft.at[part], smoothed.at[part], soft_sem.at[chunk]),
            pltpu.make_async_copy(grads.at[:, part], normals.at[:, part], grad_sem.at[chunk]),
        )

    for chunk in range(chunks):
        load(chunk).start()
    sub = lax.broadcasted_iota(I32, (full_y, size_z), 0)
    inside_y = (sub < size_y) | ((sub < size_y + HX) & (iy < ny - 1)) | ((sub >= size_y + HX) & (iy > 0))
    keep_y = jnp.where(inside_y, 0.2, 0.0)

    def one_pass(src, dst, first, end):
        def step(x, _):
            centre = src[x]
            total = (
                centre + src[x + 1] + src[x - 1]
                + pltpu.roll(centre, 1, 0) + pltpu.roll(centre, full_y - 1, 0)
            )
            inside = ((x >= HX) | (ix > 0)) & ((x < HX + size_x) | (ix < nx - 1))
            dst[x] = total * jnp.where(inside, keep_y, 0.0)
            return 0

        lax.fori_loop(first, end, step, 0, unroll=4)

    for chunk in range(chunks):
        load(chunk).wait()
        one_pass(zero, one, max(1, 8 * chunk - 1), 8 * chunk + 7)
    one_pass(one, two, 2, full_x - 2)
    one_pass(two, one, 3, full_x - 3)
    last_z = lax.broadcasted_iota(I32, (size_y, size_z), 1)

    def gradient(chunk, _):
        for k in range(8):
            x = 8 * chunk + k
            row = HX + x
            centre = one[row]
            own = centre[0:size_y]
            grad_x = one[row + 1, 0:size_y, :] - one[row - 1, 0:size_y, :]
            grad_y = (pltpu.roll(centre, full_y - 1, 0) - pltpu.roll(centre, 1, 0))[0:size_y]
            ahead = jnp.where(last_z == size_z - 1, 0.0, pltpu.roll(own, size_z - 1, 1))
            behind = jnp.where(last_z == 0, 0.0, pltpu.roll(own, 1, 1))
            grad_z = ahead - behind
            factor = lax.rsqrt(1.0 + grad_x * grad_x + grad_y * grad_y + grad_z * grad_z)
            soft[x] = own
            grads[0, x] = grad_x * factor
            grads[1, x] = grad_y * factor
            grads[2, x] = grad_z * factor
        for copy in store(chunk):
            copy.start()
        return 0

    lax.fori_loop(0, size_x // 8, gradient, 0)
    for chunk in range(size_x // 8):
        for copy in store(chunk):
            copy.wait()


def shards(density, band_feat, band_cell, band_count, w_in, w_hid, w_out, biases):
    size_x, size_y, size_z = density.shape
    feat = jnp.swapaxes(band_feat[0, 0], 1, 2)
    sides, width, listed = feat.shape
    levels, hidden = w_hid.shape[2], w_hid.shape[3]
    rows = listed // 128
    full = (size_x + 2 * HX, size_y + HY, size_z)
    beside = (size_x + 2 * HX, HY, size_z)
    hbm = pl.BlockSpec(memory_space=pltpu.HBM)
    dma = pltpu.SemaphoreType.DMA
    own_cells = (sides * rows, 128)
    message = (rows + 2 * HX, 128)
    tables = (3, 2 * full[0], 128)
    ext = pl.pallas_call(
        blend_kernel,
        out_shape=jax.ShapeDtypeStruct(full, F32),
        in_specs=[hbm] * 8,
        out_specs=hbm,
        scratch_shapes=[
            pltpu.VMEM(full, F32),
            pltpu.VMEM(beside, F32),
            pltpu.VMEM(beside, F32),
            pltpu.VMEM(full, F32),
            pltpu.VMEM(full, F32),
            pltpu.VMEM((sides, width, listed), BF16),
            pltpu.VMEM(own_cells, I32),
            pltpu.VMEM((2 * HX, 128), I32),
            pltpu.VMEM((2 * HX, 128), I32),
            pltpu.VMEM((8, 2 * HX, 128), I32),
            pltpu.VMEM((2,) + own_cells, I32),
            pltpu.VMEM(tables, I32),
            pltpu.VMEM((sides, rows, 128), F32),
            pltpu.VMEM(message, F32),
            pltpu.VMEM(message, F32),
            pltpu.VMEM(message, F32),
            pltpu.VMEM(message, F32),
            pltpu.VMEM((4, 8, 128), F32),
            pltpu.VMEM((4, 8, 128), F32),
            pltpu.VMEM((4,) + message, F32),
            pltpu.VMEM(tables, F32),
            pltpu.VMEM((sides, listed), I32),
            pltpu.SMEM((1, sides), I32),
            pltpu.VMEM((width, hidden), BF16),
            pltpu.VMEM((levels, hidden, hidden), BF16),
            pltpu.VMEM((1, hidden), BF16),
            pltpu.VMEM((levels + 1, 1, hidden), F32),
            pltpu.VMEM((hidden, width), BF16),
            pltpu.VMEM((levels, hidden, hidden), BF16),
            pltpu.VMEM((levels + 1, hidden, 128), F32),
            pltpu.VMEM((2, len(ROUTES), width // ROW_PARTS, listed * ROW_PARTS // len(ROUTES)), BF16),
            dma((7,)), dma((len(ROUTES),)), dma((len(ROUTES),)), dma((2, len(ROUTES))), dma((2, len(ROUTES))),
            dma((sides,)), dma((sides,)),
            dma((8,)), dma((8,)), dma((8,)), dma((8,)), dma((8,)), dma((8,)), dma((full[0] // 4,)),
        ],
        compiler_params=pltpu.CompilerParams(
            collective_id=0, has_side_effects=True, vmem_limit_bytes=61 << 20
        ),
        name="blend",
    )(
        density, feat, band_cell[0, 0], band_count[0], w_in[0, 0], w_hid[0, 0],
        w_out[0], biases[0, 0][:, None, :],
    )
    return pl.pallas_call(
        finish_kernel,
        out_shape=(
            jax.ShapeDtypeStruct(density.shape, F32),
            jax.ShapeDtypeStruct((3,) + density.shape, F32),
        ),
        in_specs=[hbm],
        out_specs=(hbm, hbm),
        scratch_shapes=[
            pltpu.VMEM(full, F32),
            pltpu.VMEM(full, F32),
            pltpu.VMEM(full, F32),
            pltpu.VMEM(density.shape, F32),
            pltpu.VMEM((3,) + density.shape, F32),
            dma((full[0] // 8,)), dma((size_x // 8,)), dma((size_x // 8,)),
        ],
        compiler_params=pltpu.CompilerParams(vmem_limit_bytes=61 << 20),
        name="finish",
    )(ext)


def solution(mesh):
    placed = (
        P("bx", "by", None),
        P("bx", "by", None, None, None),
        P("bx", "by", None, None),
        P("bx", "by", None),
        P("bx", "by", None, None),
        P("bx", "by", None, None, None),
        P("bx", "by", None),
        P("bx", "by", None, None),
    )
    return jax.shard_map(
        shards,
        mesh=mesh,
        in_specs=placed,
        out_specs=(P("bx", "by", None), P(None, "bx", "by", None)),
        check_vma=False,
    )
```

```python
import functools

import jax
import jax.numpy as jnp
from jax import lax
from jax.experimental import pallas as pl
from jax.experimental.pallas import tpu as pltpu
from jax.sharding import PartitionSpec as P

MESH = pl.DeviceIdType.MESH
F32, BF16, I32 = jnp.float32, jnp.bfloat16, jnp.int32
HX, HY = 4, 8
GROUP = 4
ROUTES = (2, 1, 3, 2, 0, 1, 3, 2)
ROW_PARTS = 2
AROUND = ((-1, 0), (1, 0), (0, -1), (0, 1), (-1, -1), (-1, 1), (1, -1), (1, 1))


def spread(row, index):
    wide = jnp.broadcast_to(row, index.shape)
    return jnp.take_along_axis(wide, index, axis=1, mode="promise_in_bounds")


def blend_kernel(
    dens, feat, cell, count, w_in, w_hid, w_out, bias, out,
    field, side_after, side_before, coef_x, coef_y, recv, cells, tile_lo, tile_hi, tiles_in, cells_in, table,
    nets, up, down, left, right, corner_out, corner_in, values_in, values,
    cell_v, count_s, win_v, whid_v, wout_v, bias_v, win_t, whid_t, bias_w,
    relayed, load_sem, far_send, far_recv, relay_send, relay_recv, feat_send, feat_recv, dens_send, dens_recv, cell_send, cell_recv, value_send, value_recv, out_sem,
):
    ix, iy = lax.axis_index("bx"), lax.axis_index("by")
    nx, ny = lax.axis_size("bx"), lax.axis_size("by")
    size_x, size_y, size_z = dens.shape
    listed = cell.shape[1]
    rows = listed // 128
    wide = size_x + 2 * HX
    base_2, base_3 = wide, wide + wide // 2

    def there(dx, dy):
        ok_x = jnp.bool_(True) if dx == 0 else (ix + dx >= 0 if dx < 0 else ix + dx < nx)
        ok_y = jnp.bool_(True) if dy == 0 else (iy + dy >= 0 if dy < 0 else iy + dy < ny)
        return ok_x & ok_y

    def at(dx, dy):
        return {"bx": ix + dx, "by": iy + dy}

    loads = [
        pltpu.make_async_copy(src, dst, load_sem.at[n])
        for n, (src, dst) in enumerate(
            ((cell, cell_v), (count, count_s), (w_hid, whid_v), (w_in, win_v), (w_out, wout_v), (bias, bias_v),
             (dens, field.at[pl.ds(HX, size_x), pl.ds(0, size_y), :]))
        )
    ]
    field[0:HX] = jnp.zeros_like(field[0:HX])
    field[HX + size_x :] = jnp.zeros_like(field[HX + size_x :])
    side_after[...] = jnp.zeros_like(side_after)
    side_before[...] = jnp.zeros_like(side_before)
    values_in[...] = jnp.zeros_like(values_in)
    corner_in[...] = jnp.zeros_like(corner_in)
    nets[...] = jnp.zeros_like(nets)
    tiles_in[...] = jnp.full_like(tiles_in, -1)
    cells_in[...] = jnp.full_like(cells_in, -1)
    for load in loads:
        load.start()
    place_in = ix % GROUP
    flows = []
    for step, first in ((1, GROUP - 1), (-1, 0)):
        def starts(shift, step=step, first=first):
            origin = ix + shift
            return (origin % GROUP == first) & (origin >= 0) & (origin < nx) & (origin + step >= 0) & (origin + step < nx)

        flows.append((step, 1 if step > 0 else 0, starts))
    behind = sorted({r for r in ROUTES if r})
    expected = sum(there(dx, dy).astype(I32) for dx, dy in AROUND)
    barrier = pltpu.get_barrier_semaphore()
    for dx, dy in AROUND:
        @pl.when(there(dx, dy))
        def _(dx=dx, dy=dy):
            pl.semaphore_signal(barrier, inc=1, device_id=at(dx, dy), device_id_type=MESH)

    for step, _side, starts in flows:
        for r in behind:
            if r > 1:
                @pl.when(starts(r * step))
                def _(r=r, step=step):
                    pl.semaphore_signal(barrier, inc=1, device_id=at(r * step, 0), device_id_type=MESH)

                expected = expected + starts(0).astype(I32)

            @pl.when(starts(-step))
            def _(r=r, step=step):
                pl.semaphore_signal(barrier, inc=1, device_id=at(-(r + 1) * step, 0), device_id_type=MESH)

            expected = expected + starts(r * step).astype(I32)

    loads[0].wait()
    loads[1].wait()
    ranks = lax.broadcasted_iota(I32, (1, listed), 1)
    for s in range(4):
        usable = (ranks < count_s[0, s]) & there(*AROUND[s])
        height = jnp.where(usable, cell_v[s : s + 1, :] & (size_z - 1), -1)
        for r in range(rows):
            cells[s * rows + r : s * rows + r + 1, :] = height[:, r * 128 : (r + 1) * 128]
    pairs = HX // 2
    tile_lo[0:HX] = cells[0:HX]
    tile_hi[0:HX] = cells[2 * rows - HX : 2 * rows]
    for n, s in enumerate((2, 3)):
        tile_lo[HX + n * pairs : HX + (n + 1) * pairs] = cells[s * rows : s * rows + pairs]
        tile_hi[HX + n * pairs : HX + (n + 1) * pairs] = cells[(s + 1) * rows - pairs : (s + 1) * rows]

    def fill(which, source):
        table[which, HX : HX + size_x] = source[0 : 2 * rows]
        for n, base in enumerate((base_2, base_3)):
            table[which, base + pairs : base + pairs + rows] = source[(2 + n) * rows : (3 + n) * rows]

    def fill_strips(which, lo, hi):
        table[which, 0:HX] = lo[0:HX]
        table[which, HX + size_x : wide] = hi[0:HX]
        for n, base in enumerate((base_2, base_3)):
            table[which, base : base + pairs] = lo[HX + n * pairs : HX + (n + 1) * pairs]
            table[which, base + pairs + rows : base + rows + 2 * pairs] = hi[HX + n * pairs : HX + (n + 1) * pairs]

    lane = lax.broadcasted_iota(I32, (8, 128), 1)
    sub = lax.broadcasted_iota(I32, (8, 128), 0)
    groups = size_y // 8
    half = groups // 2
    index = [4 * (8 * g + sub) + lane // 32 for g in range(groups)]
    dist_y = [((8 * g + sub).astype(F32) + 0.5) / size_y - 0.5 for g in range(groups)]
    after = sub < HX

    def both(first, second):
        return jnp.where(after, first, second)

    top = groups - 1
    index_side = both(index[0], index[top])
    index_side_y = [both(index[half * parity], index[top % half + half * parity]) for parity in range(2)]
    dist_side, off_side = both(dist_y[0], dist_y[top]), both(-1.0, 1.0)

    def entries(lists, g, pair, parity):
        def row(which, at_row):
            return lists[which, pl.ds(at_row, 1), :]

        x = 2 * pair + parity
        if g < groups:
            row_y = row(0, (base_2 if g < half else base_3) + pair)
            return spread(row(0, x), index[g]), spread(row_y, index[g % half + half * parity])
        row_x = both(row(2, x), row(1, x))
        row_y = both(row(2, base_2 + pair), row(1, base_3 + pair))
        return spread(row_x, index_side), spread(row_y, index_side_y[parity])

    def prepare(chosen):
        def step(pair, _):
            for parity in range(2):
                x = 2 * pair + parity
                local = (x + size_x - HX) % size_x
                dist_x = (local.astype(F32) + 0.5) / size_x - 0.5
                off_x = jnp.where(local < size_x // 2, -1.0, 1.0)
                for g in chosen:
                    in_x, in_y = entries(table, g, pair, parity)
                    voxels = pl.ds(8 * g, 8)
                    if g < groups:
                        across, off_y = dist_y[g], -1.0 if g < half else 1.0
                        density = field[x, voxels, :]
                    else:
                        across, off_y = dist_side, off_side
                        density = both(side_after[x], side_before[x])
                    sq_x, sq_y = dist_x * dist_x, across * across
                    far_x, far_y = dist_x - off_x, across - off_y
                    own = 1.0 / (sq_x + sq_y + 0.25)
                    w_x = jnp.where(in_x == lane, 1.0 / (far_x * far_x + sq_y + 0.25), 0.0)
                    w_y = jnp.where(in_y == lane, 1.0 / (sq_x + far_y * far_y + 0.25), 0.0)
                    share = 1.0 / (own + w_x + w_y)
                    field[x, voxels, :] = own * density * share
                    coef_x[x, voxels, :] = w_x * share
                    coef_y[x, voxels, :] = w_y * share
            return 0

        return step

    own_groups = tuple(range(groups))
    fill(0, cells)
    for load in loads[2:]:
        load.wait()
    lax.fori_loop(pairs, wide // 2 - pairs, prepare(own_groups), 0)
    for layer in range(w_hid.shape[0]):
        whid_t[layer] = whid_v[layer].T
    win_t[...] = win_v[...].T
    for layer in range(bias.shape[0]):
        bias_w[layer] = jnp.broadcast_to(bias_v[layer], (128, bias.shape[2])).T

    pl.semaphore_wait(barrier, expected)

    def remote(src, dst, send, arrive, n, dx, dy):
        return pltpu.make_async_remote_copy(
            src_ref=src, dst_ref=dst, send_sem=send.at[n], recv_sem=arrive.at[n],
            device_id=at(dx, dy), device_id_type=MESH)

    def opposite(s):
        dx = jnp.where(s == 0, 1, jnp.where(s == 1, -1, 0))
        dy = jnp.where(s == 2, 1, jnp.where(s == 3, -1, 0))
        ok = (ix + dx >= 0) & (ix + dx < nx) & (iy + dy >= 0) & (iy + dy < ny)
        return ok, dx, dy

    def feature_copy(s, dx, dy):
        return remote(feat.at[s], recv.at[s], feat_send, feat_recv, s, dx, dy)

    def density_copy(n, dx, dy):
        if dx == 0:
            src_x, dst_x = pl.ds(0, size_x), pl.ds(HX, size_x)
        elif dx > 0:
            src_x, dst_x = pl.ds(size_x - HX, HX), pl.ds(0, HX)
        else:
            src_x, dst_x = pl.ds(0, HX), pl.ds(HX + size_x, HX)
        if dy == 0:
            src, dst = dens.at[src_x], field.at[dst_x, pl.ds(0, size_y), :]
        elif dy > 0:
            src, dst = dens.at[src_x, pl.ds(size_y - HY, HY), :], side_before.at[dst_x]
        else:
            src, dst = dens.at[src_x, pl.ds(0, HY), :], side_after.at[dst_x]
        return remote(src, dst, dens_send, dens_recv, n, dx, dy)

    def cell_copy(n, dx, dy):
        m = AROUND.index((-dx, -dy))
        if dx == 0:
            return remote(cells, cells_in.at[m - 2], cell_send, cell_recv, n, dx, dy)
        return remote(tile_lo if dx < 0 else tile_hi, tiles_in.at[m], cell_send, cell_recv, n, dx, dy)

    def value_copy(n, dx, dy):
        m = AROUND.index((-dx, -dy))
        if dx and dy:
            return remote(corner_out.at[n - 4], corner_in.at[m - 4], value_send, value_recv, n, dx, dy)
        src = (left if dy < 0 else right) if dx == 0 else (down if dx < 0 else up)
        return remote(src, values_in.at[m], value_send, value_recv, n, dx, dy)

    part_rows = feat.shape[1] // ROW_PARTS
    part_columns = listed * ROW_PARTS // len(ROUTES)

    def piece(ref, s, n):
        return ref.at[
            s, pl.ds(n % ROW_PARTS * part_rows, part_rows), pl.ds(n // ROW_PARTS * part_columns, part_columns)
        ]

    def far_copy(n, side, step):
        r = ROUTES[n]
        if r:
            dst, arrive, shift = relayed.at[side, n], relay_recv.at[side, n], -r * step
        else:
            dst, arrive, shift = piece(recv, side, n), far_recv.at[n], step
        return pltpu.make_async_remote_copy(
            src_ref=piece(feat, side, n), dst_ref=dst, send_sem=far_send.at[n], recv_sem=arrive,
            device_id=at(shift, 0), device_id_type=MESH)

    def forward_copy(n, side, step):
        return pltpu.make_async_remote_copy(
            src_ref=relayed.at[side, n], dst_ref=piece(recv, side, n), send_sem=relay_send.at[side, n],
            recv_sem=far_recv.at[n], device_id=at((ROUTES[n] + 1) * step, 0), device_id_type=MESH)

    for step, side, starts in flows:
        @pl.when(starts(0))
        def _(step=step, side=side):
            for n in range(len(ROUTES)):
                far_copy(n, side, step).start()

    def near(s):
        ok = there(*AROUND[s])
        for step, side, starts in flows:
            if s == side:
                ok = ok & jnp.logical_not(starts(0))
        return ok

    for s in (2, 3, 0, 1):
        @pl.when(near(s))
        def _(s=s):
            feature_copy(s, *AROUND[s]).start()

    lower = ix < nx // 2
    for (step, side, starts), turn in ((flows[1], lower), (flows[0], True), (flows[1], jnp.logical_not(lower))):
        for n in range(len(ROUTES)):
            if ROUTES[n]:
                @pl.when(starts(ROUTES[n] * step) & turn)
                def _(n=n, step=step, side=side):
                    far_copy(n, side, step).wait_recv()
                    forward_copy(n, side, step).start()

    for n, (dx, dy) in enumerate(AROUND):
        @pl.when(there(dx, dy))
        def _(n=n, dx=dx, dy=dy):
            cell_copy(n, dx, dy).start()
            density_copy(n, dx, dy).start()

    head = jnp.broadcast_to(wout_v[...].astype(F32), (16, w_out.shape[1])).astype(BF16)
    last = ix % 4 == 3

    def evaluate(step, _):
        s = jnp.where(step < 2, step + 2, jnp.where(last, 3 - step, step - 2))
        ok, dx, dy = opposite(s)

        @pl.when(ok)
        def _():
            far = ((s == 1) & flows[0][2](-1)) | ((s == 0) & flows[1][2](1))

            @pl.when(far)
            def _():
                for n in range(len(ROUTES)):
                    pltpu.make_async_remote_copy(
                        src_ref=piece(recv, s, n), dst_ref=piece(recv, s, n), send_sem=far_send.at[n],
                        recv_sem=far_recv.at[n], device_id=at(dx, dy), device_id_type=MESH).wait_recv()

            @pl.when(jnp.logical_not(far))
            def _():
                feature_copy(s, dx, dy).wait_recv()

            def layer(weights, hidden, level):
                column = jnp.concatenate([bias_w[level]] * (listed // 128), axis=1)
                total = jnp.dot(weights, hidden, preferred_element_type=F32) + column
                return jnp.maximum(total.astype(BF16), 0)

            hidden = layer(win_t[...], recv[s], 0)
            for level in range(whid_t.shape[0]):
                hidden = layer(whid_t[level], hidden, level + 1)
            raw = jnp.dot(head, hidden, preferred_element_type=F32)[0:1, :]
            result = jnp.maximum(raw, 0.0) + jnp.log1p(jnp.exp(-jnp.abs(raw)))
            for r in range(rows):
                nets[s, r : r + 1, :] = result[:, r * 128 : (r + 1) * 128]

        return 0

    lax.fori_loop(0, 4, evaluate, 0)

    up[0:rows] = nets[0]
    down[0:rows] = nets[1]
    for n, s in enumerate((2, 3)):
        up[rows + n * pairs : rows + (n + 1) * pairs] = nets[s, rows - pairs : rows]
        down[rows + n * pairs : rows + (n + 1) * pairs] = nets[s, 0:pairs]

    def send_values(chosen):
        for n in chosen:
            @pl.when(there(*AROUND[n]))
            def _(n=n):
                value_copy(n, *AROUND[n]).start()

    send_values((0, 1))
    first_half = lax.broadcasted_iota(I32, (1, 128), 1) < 64
    for n in range(4, 8):
        dx, dy = AROUND[n]
        along, beside = (0 if dx > 0 else 1), (2 if dy > 0 else 3)
        edge = 4 * HX
        shift = 128 - edge if dy > 0 else edge
        near_edge = lane >= 128 - edge if dy > 0 else lane < edge
        corner_out[n - 4] = jnp.where(near_edge, nets[along, 0:8], pltpu.roll(nets[along, 8:16], shift, 1))
        for k in range(pairs):
            at_row = rows - pairs + k if dx > 0 else k
            line = nets[beside, at_row : at_row + 1, :]
            turned = pltpu.roll(line, 64, 1)
            kept = first_half if dy > 0 else jnp.logical_not(first_half)
            for h, value in enumerate((line, turned) if dy > 0 else (turned, line)):
                to = 2 * k + h
                corner_out[n - 4, to : to + 1, :] = jnp.where(kept, value, corner_out[n - 4, to : to + 1, :])

    send_values((4, 5, 6, 7))
    left[0:rows] = nets[3]
    right[0:rows] = nets[2]
    for side in (left, right):
        side[rows : rows + HX] = nets[0, 0:HX]
        side[rows + HX : rows + 2 * HX] = nets[1, rows - HX : rows]
    send_values((2, 3))

    def unpacked(m):
        tile = corner_in[m - 4]
        low = AROUND[m][1] < 0
        lines = []
        for k in range(pairs):
            one, two = tile[2 * k : 2 * k + 1], tile[2 * k + 1 : 2 * k + 2]
            if low:
                lines.append(jnp.where(first_half, one, pltpu.roll(two, 64, 1)))
            else:
                lines.append(jnp.where(first_half, pltpu.roll(one, 64, 1), two))
        return tile, pltpu.roll(tile, 4 * HX if low else 128 - 4 * HX, 1), lines

    for n, (dx, dy) in enumerate(AROUND):
        @pl.when(there(-dx, -dy))
        def _(n=n, dx=dx, dy=dy):
            cell_copy(n, dx, dy).wait_recv()
            density_copy(n, dx, dy).wait_recv()

    fill(1, cells_in.at[0])
    fill(2, cells_in.at[1])
    fill_strips(0, tiles_in.at[0], tiles_in.at[1])
    fill_strips(1, tiles_in.at[4], tiles_in.at[6])
    fill_strips(2, tiles_in.at[5], tiles_in.at[7])
    lax.fori_loop(0, pairs, prepare(own_groups), 0, unroll=True)
    lax.fori_loop(wide // 2 - pairs, wide // 2, prepare(own_groups), 0, unroll=True)
    lax.fori_loop(0, wide // 2, prepare((groups,)), 0, unroll=5)

    def arrived(along):
        for n, (dx, dy) in enumerate(AROUND):
            if -dx == along:
                @pl.when(there(-dx, -dy))
                def _(n=n, dx=dx, dy=dy):
                    value_copy(n, dx, dy).wait_recv()

    def put(which, first, source):
        values[which, first : first + source.shape[0]] = source

    tail, strip = HX + size_x, rows
    lo_2, hi_2 = base_2 + pairs, base_2 + pairs + rows
    lo_3, hi_3 = base_3 + pairs, base_3 + pairs + rows
    west, east, south, north = (values_in.at[m] for m in range(4))

    def put_corner(m, which, base, at_x, at_pair):
        head_rows, tail_rows, lines = unpacked(m)
        put(which, at_x, head_rows)
        put(which, at_x + 8, tail_rows)
        for k, line in enumerate(lines):
            put(0, base + at_pair + k, line)

    put(0, 0, nets[1, rows - HX : rows])
    put(0, tail, nets[0, 0:HX])
    put(1, lo_3, nets[3])
    put(2, lo_2, nets[2])
    arrived(0)
    put(0, lo_2, south[0:rows])
    put(0, lo_3, north[0:rows])
    for which, column in ((1, south), (2, north)):
        put(which, 0, column[strip + HX : strip + 2 * HX])
        put(which, tail, column[strip : strip + HX])

    def result_copy(chunk):
        part = pl.ds(4 * chunk, 4)
        return pltpu.make_async_copy(field.at[part], out.at[part], out_sem.at[chunk])

    def blend(chunk):
        for k in range(4):
            pair, parity = 2 * chunk + k // 2, k % 2
            x = 4 * chunk + k
            for g in range(groups + 1):
                from_x, from_y = entries(values, g, pair, parity)
                voxels = pl.ds(8 * g, 8)
                field[x, voxels, :] = (
                    field[x, voxels, :] + coef_x[x, voxels, :] * from_x + coef_y[x, voxels, :] * from_y
                )
        result_copy(chunk).start()

    chunks = wide // 4

    def blend_half(turn, _):
        upper = jnp.where(place_in == 0, 1 - turn, turn)

        @pl.when(upper == 0)
        def _():
            arrived(-1)
            put(0, HX, west[0:rows])
            put_corner(4, 1, base_2, HX, 0)
            put_corner(5, 2, base_3, HX, 0)
            put(1, base_3, west[strip + pairs : strip + 2 * pairs])
            put(2, base_2, west[strip : strip + pairs])

        @pl.when(upper == 1)
        def _():
            arrived(1)
            put(0, HX + rows, east[0:rows])
            put_corner(6, 1, base_2, HX + rows, pairs + rows)
            put_corner(7, 2, base_3, HX + rows, pairs + rows)
            put(1, hi_3, east[strip + pairs : strip + 2 * pairs])
            put(2, hi_2, east[strip : strip + pairs])

        def step(k, _):
            blend(chunks // 2 * upper + k)
            return 0

        lax.fori_loop(0, chunks // 2, step, 0, unroll=True)
        return 0

    lax.fori_loop(0, 2, blend_half, 0)

    for s in range(4):
        @pl.when(near(s))
        def _(s=s):
            feature_copy(s, *AROUND[s]).wait_send()

    for step, side, starts in flows:
        @pl.when(starts(0))
        def _(step=step, side=side):
            for n in range(len(ROUTES)):
                far_copy(n, side, step).wait_send()

        for n in range(len(ROUTES)):
            if ROUTES[n]:
                @pl.when(starts(ROUTES[n] * step))
                def _(n=n, step=step, side=side):
                    forward_copy(n, side, step).wait_send()

    for n, (dx, dy) in enumerate(AROUND):
        @pl.when(there(dx, dy))
        def _(n=n, dx=dx, dy=dy):
            cell_copy(n, dx, dy).wait_send()
            density_copy(n, dx, dy).wait_send()
            value_copy(n, dx, dy).wait_send()
    for chunk in range(chunks):
        result_copy(chunk).wait()


def finish_kernel(ext, smoothed, normals, zero, one, two, soft, grads, load_sem, soft_sem, grad_sem):
    ix, iy = lax.axis_index("bx"), lax.axis_index("by")
    nx, ny = lax.axis_size("bx"), lax.axis_size("by")
    size_x, size_y, size_z = smoothed.shape
    full_x, full_y = size_x + 2 * HX, size_y + HY
    chunks = full_x // 8

    def load(chunk):
        part = pl.ds(8 * chunk, 8)
        return pltpu.make_async_copy(ext.at[part], zero.at[part], load_sem.at[chunk])

    def store(chunk):
        part = pl.ds(8 * chunk, 8)
        return (
            pltpu.make_async_copy(soft.at[part], smoothed.at[part], soft_sem.at[chunk]),
            pltpu.make_async_copy(grads.at[:, part], normals.at[:, part], grad_sem.at[chunk]),
        )

    for chunk in range(chunks):
        load(chunk).start()
    sub = lax.broadcasted_iota(I32, (full_y, size_z), 0)
    inside_y = (sub < size_y) | ((sub < size_y + HX) & (iy < ny - 1)) | ((sub >= size_y + HX) & (iy > 0))
    keep_y = jnp.where(inside_y, 0.2, 0.0)

    def one_pass(src, dst, first, end):
        def step(x, _):
            centre = src[x]
            total = (
                centre + src[x + 1] + src[x - 1]
                + pltpu.roll(centre, 1, 0) + pltpu.roll(centre, full_y - 1, 0)
            )
            inside = ((x >= HX) | (ix > 0)) & ((x < HX + size_x) | (ix < nx - 1))
            dst[x] = total * jnp.where(inside, keep_y, 0.0)
            return 0

        lax.fori_loop(first, end, step, 0, unroll=4)

    for chunk in range(chunks):
        load(chunk).wait()
        one_pass(zero, one, max(1, 8 * chunk - 1), 8 * chunk + 7)
    one_pass(one, two, 2, full_x - 2)
    one_pass(two, one, 3, full_x - 3)
    last_z = lax.broadcasted_iota(I32, (size_y, size_z), 1)

    def gradient(chunk, _):
        for k in range(8):
            x = 8 * chunk + k
            row = HX + x
            centre = one[row]
            own = centre[0:size_y]
            grad_x = one[row + 1, 0:size_y, :] - one[row - 1, 0:size_y, :]
            grad_y = (pltpu.roll(centre, full_y - 1, 0) - pltpu.roll(centre, 1, 0))[0:size_y]
            ahead = jnp.where(last_z == size_z - 1, 0.0, pltpu.roll(own, size_z - 1, 1))
            behind = jnp.where(last_z == 0, 0.0, pltpu.roll(own, 1, 1))
            grad_z = ahead - behind
            factor = lax.rsqrt(1.0 + grad_x * grad_x + grad_y * grad_y + grad_z * grad_z)
            soft[x] = own
            grads[0, x] = grad_x * factor
            grads[1, x] = grad_y * factor
            grads[2, x] = grad_z * factor
        for copy in store(chunk):
            copy.start()
        return 0

    lax.fori_loop(0, size_x // 8, gradient, 0)
    for chunk in range(size_x // 8):
        for copy in store(chunk):
            copy.wait()


def shards(density, band_feat, band_cell, band_count, w_in, w_hid, w_out, biases):
    size_x, size_y, size_z = density.shape
    feat = jnp.swapaxes(band_feat[0, 0], 1, 2)
    sides, width, listed = feat.shape
    levels, hidden = w_hid.shape[2], w_hid.shape[3]
    rows = listed // 128
    full = (size_x + 2 * HX, size_y + HY, size_z)
    beside = (size_x + 2 * HX, HY, size_z)
    hbm = pl.BlockSpec(memory_space=pltpu.HBM)
    dma = pltpu.SemaphoreType.DMA
    own_cells = (sides * rows, 128)
    message = (rows + 2 * HX, 128)
    tables = (3, 2 * full[0], 128)
    ext = pl.pallas_call(
        blend_kernel,
        out_shape=jax.ShapeDtypeStruct(full, F32),
        in_specs=[hbm] * 8,
        out_specs=hbm,
        scratch_shapes=[
            pltpu.VMEM(full, F32),
            pltpu.VMEM(beside, F32),
            pltpu.VMEM(beside, F32),
            pltpu.VMEM(full, F32),
            pltpu.VMEM(full, F32),
            pltpu.VMEM((sides, width, listed), BF16),
            pltpu.VMEM(own_cells, I32),
            pltpu.VMEM((2 * HX, 128), I32),
            pltpu.VMEM((2 * HX, 128), I32),
            pltpu.VMEM((8, 2 * HX, 128), I32),
            pltpu.VMEM((2,) + own_cells, I32),
            pltpu.VMEM(tables, I32),
            pltpu.VMEM((sides, rows, 128), F32),
            pltpu.VMEM(message, F32),
            pltpu.VMEM(message, F32),
            pltpu.VMEM(message, F32),
            pltpu.VMEM(message, F32),
            pltpu.VMEM((4, 8, 128), F32),
            pltpu.VMEM((4, 8, 128), F32),
            pltpu.VMEM((4,) + message, F32),
            pltpu.VMEM(tables, F32),
            pltpu.VMEM((sides, listed), I32),
            pltpu.SMEM((1, sides), I32),
            pltpu.VMEM((width, hidden), BF16),
            pltpu.VMEM((levels, hidden, hidden), BF16),
            pltpu.VMEM((1, hidden), BF16),
            pltpu.VMEM((levels + 1, 1, hidden), F32),
            pltpu.VMEM((hidden, width), BF16),
            pltpu.VMEM((levels, hidden, hidden), BF16),
            pltpu.VMEM((levels + 1, hidden, 128), F32),
            pltpu.VMEM((2, len(ROUTES), width // ROW_PARTS, listed * ROW_PARTS // len(ROUTES)), BF16),
            dma((7,)), dma((len(ROUTES),)), dma((len(ROUTES),)), dma((2, len(ROUTES))), dma((2, len(ROUTES))),
            dma((sides,)), dma((sides,)),
            dma((8,)), dma((8,)), dma((8,)), dma((8,)), dma((8,)), dma((8,)), dma((full[0] // 4,)),
        ],
        compiler_params=pltpu.CompilerParams(
            collective_id=0, has_side_effects=True, vmem_limit_bytes=61 << 20
        ),
        name="blend",
    )(
        density, feat, band_cell[0, 0], band_count[0], w_in[0, 0], w_hid[0, 0],
        w_out[0], biases[0, 0][:, None, :],
    )
    return pl.pallas_call(
        finish_kernel,
        out_shape=(
            jax.ShapeDtypeStruct(density.shape, F32),
            jax.ShapeDtypeStruct((3,) + density.shape, F32),
        ),
        in_specs=[hbm],
        out_specs=(hbm, hbm),
        scratch_shapes=[
            pltpu.VMEM(full, F32),
            pltpu.VMEM(full, F32),
            pltpu.VMEM(full, F32),
            pltpu.VMEM(density.shape, F32),
            pltpu.VMEM((3,) + density.shape, F32),
            dma((full[0] // 8,)), dma((size_x // 8,)), dma((size_x // 8,)),
        ],
        compiler_params=pltpu.CompilerParams(vmem_limit_bytes=61 << 20),
        name="finish",
    )(ext)


def solution(mesh):
    placed = (
        P("bx", "by", None),
        P("bx", "by", None, None, None),
        P("bx", "by", None, None),
        P("bx", "by", None),
        P("bx", "by", None, None),
        P("bx", "by", None, None, None),
        P("bx", "by", None),
        P("bx", "by", None, None),
    )
    return jax.shard_map(
        shards,
        mesh=mesh,
        in_specs=placed,
        out_specs=(P("bx", "by", None), P(None, "bx", "by", None)),
        check_vma=False,
    )
```
